128 devices in a mesh: gx: 8 (over y, core), gy: 16 (over x, z).
Axes of the slice: x: 4, y: 4, z: 4, core: 2. Of those that a mesh axis runs over, the one named last changes fastest.
Arguments:
- soil_now: float32 [48, 256, 4096], P(None, 'gx', 'gy'), may hold values from -6 to 6
- soil_old: float32 [48, 256, 4096], P(None, 'gx', 'gy'), may hold values from -6 to 6
- kappa: float32 [48, 256, 4096], P(None, 'gx', 'gy'), may hold values from 0.15 to 0.3
- force_prev: float32 [256, 4096], P('gx', 'gy'), may hold values from -6 to 6
- storey_disp: float32 [32, 262144], P(None, ('gx', 'gy')), may hold values from -6 to 6
- storey_vel: float32 [32, 262144], P(None, ('gx', 'gy')), may hold values from -3 to 3
- stiffness: float32 [32, 262144], P(None, ('gx', 'gy')), may hold values from 0.03 to 0.5
- branch_flag: int32 [32, 262144], P(None, ('gx', 'gy')), may hold values from 0 to 2
- footprint_tile: int32 [262144, 1], P(('gx', 'gy')), may hold values from 0 to 127; in each aligned block of 2048 rows (0 to 2047, 2048 to 4095, ...) at most 32 rows name the same one
- footprint_cell: int32 [262144], P(('gx', 'gy')), may hold values from 0 to 8191
Outputs:
- soil_next: float32 [48, 256, 4096], P(None, 'gx', 'gy')
- soil_before: float32 [48, 256, 4096], P(None, 'gx', 'gy')
- disp_next: float32 [32, 262144], P(None, ('gx', 'gy'))
- vel_next: float32 [32, 262144], P(None, ('gx', 'gy'))
- base_shear: float32 [256, 4096], P('gx', 'gy')
The draws below stay inside these ranges and needn't reach their ends.
Inputs may be any that keep to these rules, and one draw needn't show every extreme that they name: `footprint_tile`: among the 2048 buildings of one device at most 32 stand on one tile, and in every draw some tile receives exactly 32 of them from some device.
All inputs are finite; a program needn't handle non-finite values.
Results may differ from the reference program's by a relative error of at most 0.00023.
Values sent between devices are 32-bit elements; how exact they have to be, the bound alone decides.
A program may use at most 128 MiB of HBM per device.

```python
import math
import jax
import jax.numpy as jnp
import numpy as np

CX = 32
CY = 256
NZ = 48
STEPS = 8
STOREYS = 32
B_DEV = 2048
NX = 256
NY = 4096
NB = 262144
N_GX = 8
N_GY = 16


def touch_ends(values, stream_key, low, largest):
    shape = values.shape
    spot = [jax.random.randint(jax.random.fold_in(stream_key, axis), (), 0, shape[axis]) for axis in range(len(shape))]
    values = values.at[tuple(spot)].set(low)
    longest = shape.index(max(shape))
    spot[longest] = (spot[longest] + 1) % shape[longest]
    return values.at[tuple(spot)].set(largest)


def levels(rng, shape, cuts, smallest, top_value):
    def one(dim, parts):
        steps = jax.random.uniform(jax.random.fold_in(jax.random.fold_in(rng, 6), dim), (parts,), jnp.float32, smallest / len(cuts), top_value / len(cuts))
        return jnp.repeat(jnp.exp(steps), shape[dim] // parts).reshape((-1,) + (1,) * (len(shape) - dim - 1))

    gain = one(*cuts[0])
    for cut in cuts[1:]:
        gain = gain * one(*cut)
    return gain


def shared_out(own_key, own, number, rows, amount, top, most, slope):
    ranking = jax.random.permutation(own_key, amount)
    packed, ordinary = shares(amount, rows * top, most, slope, True), shares(amount, rows * top, most, slope, False)
    places = jnp.arange(amount)

    def named(tallies, turn):
        used = int((tallies > 0).sum())
        fixed = max(1, used // 4)
        moved = fixed + (places - fixed + turn * (used - fixed)) % max(1, amount - fixed)
        return jnp.zeros((amount,), jnp.int32).at[ranking[jnp.where(places < fixed, places, moved)]].set(jnp.asarray(tallies, jnp.int32))

    tallies = jnp.where(number % 4 == 0, named(packed, number // 4), named(ordinary, number - number // 4 - 1))
    mixed = jax.random.permutation(jax.random.fold_in(own, 3), amount)
    source_of, receiver = mixed[0:amount // 2 * 2:2], mixed[1:amount // 2 * 2:2]
    slack = jnp.minimum(tallies[source_of] - 1, most - tallies[receiver]) // 2
    slack = jnp.where((source_of == ranking[0]) | (receiver == ranking[0]) | (tallies[receiver] == 0), 0, jnp.maximum(slack, 0))
    moved = jax.random.randint(jax.random.fold_in(own, 4), (amount // 2,), 0, 1 << 20) % (slack + 1)
    tallies = tallies.at[source_of].add(-moved).at[receiver].add(moved)
    labels = jnp.searchsorted(jnp.cumsum(tallies), jnp.arange(rows * top), side="right").astype(jnp.int32)
    grid = labels.reshape(top, rows).T
    grid = grid[jax.random.permutation(jax.random.fold_in(own, 1), rows)]
    turn = jax.random.randint(jax.random.fold_in(own, 2), (rows, 1), 0, top)
    return jnp.take_along_axis(grid, (jnp.arange(top)[None, :] + turn) % top, axis=1)


def shares(number_of, total, bound, skew, full):
    weights = [(1 << 20) // math.isqrt(standing ** skew) + 1 for standing in range(1, number_of + 1)]
    largest = bound if full else min(bound, max(-(-total // number_of), total * weights[0] // sum(weights)))
    least = 1 if total - largest >= number_of - 1 else 0
    counts, surplus = [largest] + [least] * (number_of - 1), total - largest - least * (number_of - 1)
    while surplus > 0:
        free = [i for i in range(1, number_of) if counts[i] < largest] or [i for i in range(1, number_of) if counts[i] < bound]
        whole, budget = sum([weights[i] for i in free]), surplus
        for i in free:
            more = min(bound - counts[i], max(1, budget * weights[i] // whole), surplus)
            counts[i] = counts[i] + more
            surplus = surplus - more
    return np.array(counts)


def centred(stream_key, dims, deviation, most, pieces=(), kind=jnp.bfloat16):
    drawn = jax.random.normal(stream_key, dims, jnp.float32) * deviation
    if len(pieces) > 0:
        drawn = levels(stream_key, dims, pieces, -0.22, 0.18) * drawn
    return jnp.clip(drawn, min=-most, max=most).astype(kind)


def setup_inputs(seed: int = 0) -> dict:
    splits = jax.random.split(jax.random.key(seed), 11)
    soil_now = centred(splits[0], (NZ, NX, NY), 1.0, 6.0, ((1, 8), (2, 16)), jnp.float32)
    soil_old = centred(splits[1], (NZ, NX, NY), 1.0, 6.0, ((1, 8), (2, 16)), jnp.float32)
    kappa = jnp.clip(jnp.exp(math.log(0.3) - 0.6931472 * jax.random.uniform(splits[2], (NZ, NX, NY), jnp.float32) ** levels(splits[2], (NZ, NX, NY), ((1, 8), (2, 16)), -0.2, 0.2)), 0.15, 0.3)
    force_prev = centred(splits[3], (NX, NY), 1.0, 6.0, ((0, 8), (1, 16)), jnp.float32)
    storey_disp = centred(splits[4], (STOREYS, NB), 1.0, 6.0, ((1, 128),), jnp.float32)
    storey_vel = centred(splits[5], (STOREYS, NB), 0.5, 3.0, ((1, 128),), jnp.float32)
    stiffness = jnp.clip(jnp.exp(math.log(0.5) - 2.8134107 * jax.random.uniform(splits[6], (STOREYS, NB), jnp.float32) ** levels(splits[6], (STOREYS, NB), ((1, 128),), -0.2, 0.2)), 0.03, 0.5)
    branch_flag = touch_ends(jax.random.randint(splits[7], (STOREYS, NB), 0, 3), jax.random.fold_in(splits[7], 1), 0, 2).astype(jnp.int32)
    footprint_tile_keys = jax.random.split(jax.random.fold_in(splits[8], 1), NB // B_DEV)
    footprint_tile_turns = jax.random.permutation(jax.random.fold_in(splits[8], 3), NB // B_DEV)
    footprint_tile = jax.vmap(lambda own, number: shared_out(jax.random.fold_in(splits[8], 2), own, number, B_DEV, N_GX * N_GY, 1, 2 * B_DEV // (N_GX * N_GY), 2))(footprint_tile_keys, footprint_tile_turns).reshape((NB, 1))
    footprint_cell = touch_ends(jax.random.randint(splits[9], (NB,), 0, CX * CY), jax.random.fold_in(splits[9], 1), 0, (CX * CY) - 1).astype(jnp.int32)
    return dict(soil_now=soil_now, soil_old=soil_old, kappa=kappa, force_prev=force_prev, storey_disp=storey_disp, storey_vel=storey_vel, stiffness=stiffness, branch_flag=branch_flag, footprint_tile=footprint_tile, footprint_cell=footprint_cell)


force_gain = 0.05


def soil_advance(padded, previous, kappa, force):
    centre = padded[:, 1:-1, 1:-1]
    along_x = padded[:, :-2, 1:-1] + padded[:, 2:, 1:-1] - 2.0 * centre
    along_y = padded[:, 1:-1, :-2] + padded[:, 1:-1, 2:] - 2.0 * centre
    above = jnp.concatenate([centre[:1], centre[:-1]], 0)
    below = jnp.concatenate([centre[1:], jnp.zeros_like(centre[:1])], 0)
    vertical = above + below - 2.0 * centre
    fresh = 2.0 * centre - previous + kappa * (along_x + along_y + vertical)
    return fresh.at[0].add(force_gain * force)


def effective_stiffness(stiffness, branch_flag):
    factor = jnp.where(branch_flag == 0, 1.0, jnp.where(branch_flag == 1, 0.6, 0.15)).astype(jnp.float32)
    return stiffness * factor


def building_window(disp, vel, stiff_eff, ground):
    total = jnp.zeros(disp.shape[1], jnp.float32)
    for moment in range(ground.shape[0]):
        beneath = jnp.concatenate([ground[moment][None], disp[:-1]], 0)
        shear = stiff_eff * (disp - beneath)
        upper = jnp.concatenate([shear[1:], jnp.zeros_like(shear[:1])], 0)
        vel = vel + upper - shear
        disp = disp + vel
        total = total + shear[0]
    return disp, vel, total / ground.shape[0]


def reference(soil_now, soil_old, kappa, force_prev, storey_disp, storey_vel, stiffness, branch_flag, footprint_tile, footprint_cell):
    layers = []
    for moment in range(STEPS):
        padded = jnp.pad(soil_now, ((0, 0), (1, 1), (1, 1)))
        fresh = soil_advance(padded, soil_old, kappa, force_prev)
        soil_old, soil_now = soil_now, fresh
        layers.append(soil_now[0])
    history = jnp.stack(layers)
    target = footprint_tile[:, 0]
    row_cell = (target // N_GY) * CX + footprint_cell // CY
    col_cell = (target % N_GY) * CY + footprint_cell % CY
    ground = history[:, row_cell, col_cell]
    stiff_eff = effective_stiffness(stiffness, branch_flag)
    disp_next, vel_next, mean_shear = building_window(storey_disp, storey_vel, stiff_eff, ground)
    base_shear = jnp.zeros((NX, NY), jnp.float32).at[row_cell, col_cell].add(mean_shear)
    return soil_now, soil_old, disp_next, vel_next, base_shear
```

```python
import functools

import jax
import jax.numpy as jnp
from jax import lax
from jax.experimental import pallas as pl
from jax.experimental.pallas import tpu as pltpu
from jax.sharding import PartitionSpec as P

STEPS = 8
force_gain = 0.05
f32, bf16 = jnp.float32, jnp.bfloat16
CHUNKS = 2
SLOTS = 32
COEF, BASE, ROW, COL, WIDE = 0, 256, 288, 320, 384
BLOCK = 256
MESH = pl.DeviceIdType.MESH


def split(x):
    high = x.astype(bf16)
    return high, (x - high.astype(f32)).astype(bf16)


def nt(a, b):
    return lax.dot_general(a, b, (((1,), (1,)), ((), ())), preferred_element_type=f32)


def nn(a, b):
    return jnp.dot(a, b, preferred_element_type=f32)


def kernel(
    n_gx,
    n_gy,
    depth,
    rows,
    tile_ref,
    cell_ref,
    now_hbm,
    old_hbm,
    kappa_hbm,
    force_hbm,
    disp_hbm,
    vel_hbm,
    stiff_hbm,
    flag_hbm,
    next_hbm,
    before_hbm,
    disp_out,
    vel_out,
    base_out,
    soil_a,
    soil_b,
    kappa,
    force,
    disp,
    vel,
    stiff,
    flag,
    disp_new,
    vel_new,
    base,
    x_send,
    x_recv,
    y_send,
    y_recv,
    marks,
    rank_ref,
    payload,
    recv_one,
    mid_one,
    request,
    request_t,
    hot,
    motion,
    picked,
    reply,
    recv_two,
    mid_two,
    answer,
    in_sem,
    out_sem,
    halo_send,
    halo_recv,
    one_send,
    one_recv,
    two_send,
    two_recv,
    three_send,
    three_recv,
    four_send,
    four_recv,
):
    gx, gy = lax.axis_index("gx"), lax.axis_index("gy")
    tiles = n_gx * n_gy
    count = tile_ref.shape[1]
    planes = depth // CHUNKS
    cells = depth * rows

    loads = []
    pairs = (
        (now_hbm, soil_a.at[pl.ds(0, cells)]),
        (old_hbm, soil_b.at[pl.ds(0, cells)]),
        (kappa_hbm, kappa),
        (force_hbm, force),
        (disp_hbm, disp),
        (vel_hbm, vel),
        (stiff_hbm, stiff),
        (flag_hbm, flag),
    )
    for i, (source, target) in enumerate(pairs):
        copy = pltpu.make_async_copy(source, target, in_sem.at[i])
        copy.start()
        loads.append(copy)

    barrier = pltpu.get_barrier_semaphore()
    for k in range(1, n_gx):
        pl.semaphore_signal(
            barrier, inc=1, device_id=(lax.rem(gx + k, n_gx), gy), device_id_type=MESH
        )
    for k in range(1, n_gy):
        pl.semaphore_signal(
            barrier, inc=1, device_id=(gx, lax.rem(gy + k, n_gy)), device_id_type=MESH
        )

    soil_a[pl.ds(cells, rows), :] = jnp.zeros((rows, 256), f32)
    soil_b[pl.ds(cells, rows), :] = jnp.zeros((rows, 256), f32)
    has = (gx > 0, gx < n_gx - 1, gy > 0, gy < n_gy - 1)
    for side in range(4):

        @pl.when(jnp.logical_not(has[side]))
        def _():
            if side < 2:
                x_recv[:, side] = jnp.zeros((STEPS, 2, depth, 128), f32)
            else:
                y_recv[:, :, side - 2] = jnp.zeros((STEPS, CHUNKS, rows, 128), f32)

    neighbour = ((gx - 1, gy), (gx + 1, gy), (gx, gy - 1), (gx, gy + 1))

    def halo(slot, chunk, side):
        other = side ^ 1
        if side < 2:
            source = x_send.at[slot, side, :, pl.ds(chunk * planes, planes)]
            target = x_recv.at[slot, other, :, pl.ds(chunk * planes, planes)]
        else:
            source = y_send.at[slot, chunk, side - 2]
            target = y_recv.at[slot, chunk, other - 2]
        return pltpu.make_async_remote_copy(
            src_ref=source,
            dst_ref=target,
            send_sem=halo_send.at[slot, chunk, side],
            recv_sem=halo_recv.at[slot, chunk, other],
            device_id=neighbour[side],
            device_id_type=MESH,
        )

    def arrival(slot, chunk, side):
        if side < 2:
            target = x_recv.at[slot, side, :, pl.ds(chunk * planes, planes)]
        else:
            target = y_recv.at[slot, chunk, side - 2]
        return pltpu.make_async_remote_copy(
            src_ref=target,
            dst_ref=target,
            send_sem=halo_send.at[slot, chunk, side],
            recv_sem=halo_recv.at[slot, chunk, side],
            device_id=neighbour[side],
            device_id_type=MESH,
        )

    def send_halo(slot, chunk):
        for side in range(4):

            @pl.when(has[side])
            def _():
                halo(slot, chunk, side).start()

    def wait_halo(slot, chunk):
        for side in range(4):

            @pl.when(has[side])
            def _():
                arrival(slot, chunk, side).wait_recv()

    def edge_rows(slot, z, i, value):
        x_send[slot, 0, i, pl.ds(z, 1), :] = value[0:1]
        x_send[slot, 1, i, pl.ds(z, 1), :] = value[rows - 1 : rows]

    lane = lax.broadcasted_iota(jnp.int32, (rows, 128), 1)
    line = lax.broadcasted_iota(jnp.int32, (rows, 128), 0)

    def pack(edges, z, low, high):
        return (
            jnp.where(lane == z, jnp.broadcast_to(low[:, 0:1], (rows, 128)), edges[0]),
            jnp.where(lane == z, jnp.broadcast_to(high[:, 127:128], (rows, 128)), edges[1]),
        )

    def plane(z):
        return pl.ds(pl.multiple_of(z * rows, rows), rows)

    def advance_plane(slot, chunk, here, there, z, edges, top):
        above_z = 0 if top else z - 1
        fresh = []
        halves = [here[plane(z), 0:128], here[plane(z), 128:256]]
        turned = [pltpu.roll(half, 1, 1) for half in halves]
        back = [pltpu.roll(half, 127, 1) for half in halves]
        west = pltpu.roll(y_recv[slot, chunk, 0], 128 - z, 1)
        east = pltpu.roll(y_recv[slot, chunk, 1], 127 - z, 1)
        lows = [jnp.where(lane == 0, west, turned[0]), jnp.where(lane == 0, turned[0], turned[1])]
        highs = [jnp.where(lane == 127, back[1], back[0]), jnp.where(lane == 127, east, back[1])]
        for i in range(2):
            cols = pl.ds(i * 128, 128)
            centre = halves[i]
            north = jnp.where(
                line == 0, x_recv[slot, 0, i, pl.ds(z, 1), :], pltpu.roll(centre, 1, 0)
            )
            south = jnp.where(
                line == rows - 1,
                x_recv[slot, 1, i, pl.ds(z, 1), :],
                pltpu.roll(centre, rows - 1, 0),
            )
            above = here[plane(above_z), cols]
            below = here[plane(z + 1), cols]
            spread = (north + south) + (lows[i] + highs[i]) + (above + below) - 6.0 * centre
            value = 2.0 * centre - there[plane(z), cols] + kappa[plane(z), cols] * spread
            if top:
                value = value + force_gain * force[:, cols]
            there[plane(z), cols] = value
            if slot < STEPS - 1:
                edge_rows(slot + 1, z, i, value)
            fresh.append(value)
            if top:
                motion[i, pl.ds(slot, rows, stride=STEPS), :] = value
        return pack(edges, z, fresh[0], fresh[1])

    def advance(step, chunk, here, there):
        wait_halo(step, chunk)
        first = chunk * planes
        edges = (jnp.zeros((rows, 128), f32), jnp.zeros((rows, 128), f32))
        if chunk == 0:
            edges = advance_plane(step, chunk, here, there, 0, edges, True)
        edges = lax.fori_loop(
            max(first, 1),
            first + planes,
            lambda z, kept: advance_plane(step, chunk, here, there, z, kept, False),
            edges,
        )
        if step < STEPS - 1:
            y_send[step + 1, chunk, 0] = edges[0]
            y_send[step + 1, chunk, 1] = edges[1]
            send_halo(step + 1, chunk)

    loads[0].wait()
    for chunk in range(CHUNKS):
        first = chunk * planes

        def first_edges(z, kept):
            low, high = soil_a[plane(z), 0:128], soil_a[plane(z), 128:256]
            edge_rows(0, z, 0, low)
            edge_rows(0, z, 1, high)
            return pack(kept, z, low, high)

        edges = lax.fori_loop(
            first,
            first + planes,
            first_edges,
            (jnp.zeros((rows, 128), f32), jnp.zeros((rows, 128), f32)),
        )
        y_send[0, chunk, 0] = edges[0]
        y_send[0, chunk, 1] = edges[1]
    pl.semaphore_wait(barrier, n_gx + n_gy - 2)
    for chunk in range(CHUNKS):
        send_halo(0, chunk)

    for copy in loads[4:]:
        copy.wait()
    stiff[...] = stiff[...] * jnp.where(
        flag[...] == 0, 1.0, jnp.where(flag[...] == 1, 0.6, 0.15)
    ).astype(f32)
    payload[...] = jnp.zeros((tiles, WIDE), f32)
    before = (
        lax.broadcasted_iota(jnp.int32, (BLOCK, BLOCK), 0)
        < lax.broadcasted_iota(jnp.int32, (BLOCK, BLOCK), 1)
    ).astype(f32).astype(bf16)
    tile_number = lax.broadcasted_iota(jnp.int32, (tiles, BLOCK), 0)
    slot_number = lax.broadcasted_iota(jnp.int32, (SLOTS, BLOCK), 0)
    storey = lax.broadcasted_iota(jnp.int32, (8, BLOCK), 0)

    def list_block(j, used):
        cols = pl.ds(pl.multiple_of(j * BLOCK, BLOCK), BLOCK)
        chosen = (tile_number == tile_ref[:, cols]).astype(f32)
        mark = chosen.astype(bf16)
        marks[:, cols] = mark
        earlier = nn(mark, before) + used
        rank = jnp.sum(chosen * earlier, 0, keepdims=True).astype(jnp.int32)
        rank_ref[:, cols] = rank
        k = stiff[0:8, cols]
        of_disp = jnp.zeros((8, BLOCK), f32)
        of_vel = jnp.zeros((8, BLOCK), f32)
        coefs = jnp.zeros((8, BLOCK), f32)
        for step in reversed(range(STEPS)):
            of_vel = of_vel + of_disp
            pull = k * (jnp.where(storey == 0, 1.0, pltpu.roll(of_vel, 1, 0)) - of_vel)
            of_disp = of_disp + pull - jnp.where(storey == 7, 0.0, pltpu.roll(pull, 7, 0))
            coefs = jnp.where(storey == step, -pull[0:1], coefs)
        scale = 1.0 / STEPS
        constant = scale * jnp.sum(
            of_disp * disp[0:8, cols] + of_vel * vel[0:8, cols], 0, keepdims=True
        )
        coefs = scale * coefs
        row = (cell_ref[:, cols] // 256).astype(f32)
        col = (cell_ref[:, cols] % 256).astype(f32)
        here = slot_number == rank

        def spread_out(coef, single):
            parts = [jnp.where(rank == d, coef, 0.0) for d in range(SLOTS)]
            parts += [jnp.where(here, value, 0.0) for value in single]
            parts.append(jnp.zeros((SLOTS * (4 - len(single)), BLOCK), f32))
            return jnp.concatenate(parts, 0).astype(bf16)

        coef_high = coefs.astype(bf16).astype(f32)
        constant_high = constant.astype(bf16).astype(f32)
        payload[...] += nt(mark, spread_out(coef_high, (constant_high, row, col))) + nt(
            mark, spread_out(coefs - coef_high, (constant - constant_high,))
        )
        return used + jnp.sum(chosen, 1, keepdims=True)

    lax.fori_loop(0, count // BLOCK, list_block, jnp.zeros((tiles, 1), f32))

    def along_x(k):
        return lax.rem(gx + k, n_gx)

    def along_y(k):
        return lax.rem(gy + k, n_gy)

    def stage_x(source_of, target, send_sem, recv_sem):
        copies = []
        for k in range(1, n_gx):
            peer = along_x(k)
            copy = pltpu.make_async_remote_copy(
                src_ref=source_of(peer),
                dst_ref=target.at[gx],
                send_sem=send_sem.at[k],
                recv_sem=recv_sem.at[k],
                device_id=(peer, gy),
                device_id_type=MESH,
            )
            copy.start()
            copies.append(copy)
        return copies

    def stage_y(source_of, target, send_sem, recv_sem):
        copies = []
        for k in range(1, n_gy):
            peer = along_y(k)
            copy = pltpu.make_async_remote_copy(
                src_ref=source_of(peer),
                dst_ref=target.at[gy],
                send_sem=send_sem.at[k],
                recv_sem=recv_sem.at[k],
                device_id=(gx, peer),
                device_id_type=MESH,
            )
            copy.start()
            copies.append(copy)
        return copies

    def arrived_x(target, send_sem, recv_sem):
        for k in range(1, n_gx):
            place = target.at[lax.rem(gx + n_gx - k, n_gx)]
            pltpu.make_async_remote_copy(
                src_ref=place,
                dst_ref=place,
                send_sem=send_sem.at[k],
                recv_sem=recv_sem.at[k],
                device_id=(along_x(k), gy),
                device_id_type=MESH,
            ).wait_recv()

    def arrived_y(target, send_sem, recv_sem):
        for k in range(1, n_gy):
            place = target.at[lax.rem(gy + n_gy - k, n_gy)]
            pltpu.make_async_remote_copy(
                src_ref=place,
                dst_ref=place,
                send_sem=send_sem.at[k],
                recv_sem=recv_sem.at[k],
                device_id=(gx, along_y(k)),
                device_id_type=MESH,
            ).wait_recv()

    sends = []
    sends += stage_x(
        lambda peer: payload.at[pl.ds(pl.multiple_of(peer * n_gy, n_gy), n_gy)],
        recv_one,
        one_send,
        one_recv,
    )
    recv_one[gx] = payload[pl.ds(pl.multiple_of(gx * n_gy, n_gy), n_gy), :]

    states = (soil_a, soil_b)

    def soil_step(step):
        for chunk in range(CHUNKS):
            advance(step, chunk, states[step % 2], states[(step + 1) % 2])

    for copy in loads[1:4]:
        copy.wait()
    soil_step(0)
    soil_step(1)

    arrived_x(recv_one, one_send, one_recv)
    for q in range(n_gy):
        for s in range(n_gx):
            mid_one[q, pl.ds(s, 1), :] = recv_one[s, pl.ds(q, 1), :]
    sends += stage_y(lambda peer: mid_one.at[peer], request, two_send, two_recv)
    request[gy] = mid_one[gy]

    soil_step(2)
    soil_step(3)

    arrived_y(request, two_send, two_recv)
    for q in range(WIDE // 128):
        request_t[pl.ds(q * 128, 128), :] = (
            request[:, :, pl.ds(q * 128, 128)].reshape(tiles, 128).T
        )
    column_number = lax.broadcasted_iota(jnp.int32, (256, 128), 0).astype(f32)

    def make_hot(d, unused):
        wanted = request_t[pl.ds(COL + d, 1), :]
        hot[:, pl.ds(pl.multiple_of(d * 128, 128), 128)] = (
            (column_number == wanted).astype(f32).astype(bf16)
        )
        return unused

    lax.fori_loop(0, SLOTS, make_hot, 0)

    for step in range(4, STEPS):
        soil_step(step)
    final = states[STEPS % 2]
    stores = [
        pltpu.make_async_copy(final.at[pl.ds(0, cells)], next_hbm, out_sem.at[0]),
        pltpu.make_async_copy(
            states[(STEPS + 1) % 2].at[pl.ds(0, cells)], before_hbm, out_sem.at[1]
        ),
    ]
    for copy in stores:
        copy.start()

    table = jnp.concatenate(split(jnp.concatenate([motion[0], motion[1]], 1)), 1)
    line_number = lax.broadcasted_iota(jnp.int32, (rows, 128), 0).astype(f32)

    def pick(pair, unused):
        cols = pl.ds(pl.multiple_of(pair * 256, 256), 256)
        chosen = hot[:, cols]
        found = nn(table, jnp.concatenate([chosen, chosen], 0))
        for half in range(2):
            d = pair * 2 + half
            wanted = request_t[pl.ds(ROW + d, 1), :]
            total = jnp.zeros((STEPS, 128), f32)
            for r in range(rows):
                total += jnp.where(
                    wanted == float(r),
                    found[r * STEPS : (r + 1) * STEPS, half * 128 : (half + 1) * 128],
                    0.0,
                )
            picked[pl.ds(pl.multiple_of(d * STEPS, STEPS), STEPS), :] = total
        return unused

    lax.fori_loop(0, SLOTS // 2, pick, 0)
    for q in range(2):
        reply[:, :, pl.ds(q * 128, 128)] = (
            picked[pl.ds(q * 128, 128), :].T.reshape(n_gy, n_gx, 128)
        )
    sends += stage_y(lambda peer: reply.at[peer], recv_two, three_send, three_recv)
    recv_two[gy] = reply[gy]

    def land(pair, total):
        cols = pl.ds(pl.multiple_of(pair * 256, 256), 256)
        parts = []
        for half in range(2):
            d = pair * 2 + half
            eight = pl.ds(pl.multiple_of(d * STEPS, STEPS), STEPS)
            mean = request_t[pl.ds(BASE + d, 1), :] + jnp.sum(
                request_t[eight, :] * picked[eight, :], 0, keepdims=True
            )
            parts.append(jnp.where(line_number == request_t[pl.ds(ROW + d, 1), :], mean, 0.0))
        values = jnp.concatenate(parts, 1)
        return total + nt(jnp.concatenate(split(values), 0), hot[:, cols])

    landed = lax.fori_loop(0, SLOTS // 2, land, jnp.zeros((2 * rows, 256), f32))
    base[...] = landed[:rows] + landed[rows:]
    stores.append(pltpu.make_async_copy(base, base_out, out_sem.at[2]))
    stores[-1].start()

    arrived_y(recv_two, three_send, three_recv)
    for s in range(n_gx):
        for q in range(n_gy):
            mid_two[s, pl.ds(q, 1), :] = recv_two[q, pl.ds(s, 1), :]
    sends += stage_x(lambda peer: mid_two.at[peer], answer, four_send, four_recv)
    answer[gx] = mid_two[gx]
    arrived_x(answer, four_send, four_recv)

    answer_t = jnp.concatenate(
        [answer[:, :, pl.ds(q * 128, 128)].reshape(tiles, 128).T for q in range(2)], 0
    )
    decoded = jnp.concatenate(split(answer_t), 1)
    level = lax.broadcasted_iota(jnp.int32, (32, BLOCK), 0)

    def window(j, unused):
        cols = pl.ds(pl.multiple_of(j * BLOCK, BLOCK), BLOCK)
        mark = marks[:, cols]
        found = nn(decoded, jnp.concatenate([mark, mark], 0))
        rank = rank_ref[:, cols]
        ground = jnp.zeros((STEPS, BLOCK), f32)
        for d in range(SLOTS):
            ground += jnp.where(rank == d, found[d * STEPS : (d + 1) * STEPS], 0.0)
        k, place, speed = stiff[:, cols], disp[:, cols], vel[:, cols]
        for step in range(STEPS):
            beneath = jnp.where(level == 0, ground[step : step + 1], pltpu.roll(place, 1, 0))
            shear = k * (place - beneath)
            upper = jnp.where(level == 31, 0.0, pltpu.roll(shear, 31, 0))
            speed = speed + upper - shear
            place = place + speed
        disp_new[:, cols] = place
        vel_new[:, cols] = speed
        return unused

    lax.fori_loop(0, count // BLOCK, window, 0)
    stores.append(pltpu.make_async_copy(disp_new, disp_out, out_sem.at[3]))
    stores.append(pltpu.make_async_copy(vel_new, vel_out, out_sem.at[4]))
    for copy in stores[3:]:
        copy.start()
    for copy in sends:
        copy.wait_send()
    for slot in range(STEPS):
        for chunk in range(CHUNKS):
            for side in range(4):

                @pl.when(has[side])
                def _():
                    halo(slot, chunk, side).wait_send()

    for copy in stores:
        copy.wait()


def shards(
    soil_now,
    soil_old,
    kappa,
    force_prev,
    storey_disp,
    storey_vel,
    stiffness,
    branch_flag,
    footprint_tile,
    footprint_cell,
):
    n_gx, n_gy = lax.axis_size("gx"), lax.axis_size("gy")
    depth, rows, wide = soil_now.shape
    storeys, count = storey_disp.shape
    tiles = n_gx * n_gy
    flat = (depth * rows, wide)
    any_space = pl.BlockSpec(memory_space=pl.ANY)
    dma = pltpu.SemaphoreType.DMA
    vm = pltpu.VMEM
    out = pl.pallas_call(
        functools.partial(kernel, n_gx, n_gy, depth, rows),
        out_shape=(
            jax.ShapeDtypeStruct(flat, f32),
            jax.ShapeDtypeStruct(flat, f32),
            jax.ShapeDtypeStruct((storeys, count), f32),
            jax.ShapeDtypeStruct((storeys, count), f32),
            jax.ShapeDtypeStruct((rows, wide), f32),
        ),
        in_specs=[pl.BlockSpec(memory_space=pltpu.VMEM)] * 2 + [any_space] * 8,
        out_specs=(any_space,) * 5,
        scratch_shapes=[
            vm((flat[0] + rows, wide), f32),
            vm((flat[0] + rows, wide), f32),
            vm(flat, f32),
            vm((rows, wide), f32),
            vm((storeys, count), f32),
            vm((storeys, count), f32),
            vm((storeys, count), f32),
            vm((storeys, count), jnp.int32),
            vm((storeys, count), f32),
            vm((storeys, count), f32),
            vm((rows, wide), f32),
            vm((STEPS, 2, 2, depth, 128), f32),
            vm((STEPS, 2, 2, depth, 128), f32),
            vm((STEPS, CHUNKS, 2, rows, 128), f32),
            vm((STEPS, CHUNKS, 2, rows, 128), f32),
            vm((tiles, count), bf16),
            vm((1, count), jnp.int32),
            vm((tiles, WIDE), f32),
            vm((n_gx, n_gy, WIDE), f32),
            vm((n_gy, n_gx, WIDE), f32),
            vm((n_gy, n_gx, WIDE), f32),
            vm((WIDE, tiles), f32),
            vm((wide, SLOTS * tiles), bf16),
            vm((2, rows * STEPS, 128), f32),
            vm((SLOTS * STEPS, tiles), f32),
            vm((n_gy, n_gx, SLOTS * STEPS), f32),
            vm((n_gy, n_gx, SLOTS * STEPS), f32),
            vm((n_gx, n_gy, SLOTS * STEPS), f32),
            vm((n_gx, n_gy, SLOTS * STEPS), f32),
            dma((8,)),
            dma((5,)),
            dma((STEPS, CHUNKS, 4)),
            dma((STEPS, CHUNKS, 4)),
            dma((n_gx,)),
            dma((n_gx,)),
            dma((n_gy,)),
            dma((n_gy,)),
            dma((n_gy,)),
            dma((n_gy,)),
            dma((n_gx,)),
            dma((n_gx,)),
        ],
        compiler_params=pltpu.CompilerParams(
            collective_id=0, has_side_effects=True, vmem_limit_bytes=40 * 1024 * 1024
        ),
        cost_estimate=pl.CostEstimate(
            flops=4_000_000_000, bytes_accessed=10_000_000, transcendentals=0
        ),
    )(
        footprint_tile.reshape(1, count),
        footprint_cell.reshape(1, count),
        soil_now.reshape(flat),
        soil_old.reshape(flat),
        kappa.reshape(flat),
        force_prev,
        storey_disp,
        storey_vel,
        stiffness,
        branch_flag,
    )
    return (
        out[0].reshape(soil_now.shape),
        out[1].reshape(soil_now.shape),
        out[2],
        out[3],
        out[4],
    )


def solution(mesh):
    return jax.shard_map(
        shards,
        mesh=mesh,
        in_specs=(
            P(None, "gx", "gy"),
            P(None, "gx", "gy"),
            P(None, "gx", "gy"),
            P("gx", "gy"),
            P(None, ("gx", "gy")),
            P(None, ("gx", "gy")),
            P(None, ("gx", "gy")),
            P(None, ("gx", "gy")),
            P(("gx", "gy"), None),
            P(("gx", "gy")),
        ),
        out_specs=(
            P(None, "gx", "gy"),
            P(None, "gx", "gy"),
            P(None, ("gx", "gy")),
            P(None, ("gx", "gy")),
            P("gx", "gy"),
        ),
        check_vma=False,
    )
```

```python
import functools

import jax
import jax.numpy as jnp
from jax import lax
from jax.experimental import pallas as pl
from jax.experimental.pallas import tpu as pltpu
from jax.sharding import PartitionSpec as P

STEPS = 8
force_gain = 0.05
f32, bf16 = jnp.float32, jnp.bfloat16
GROUP = 4
PAD = 8
SLOTS = 32
COEF, BASE, ROW, COL, WIDE = 0, 256, 288, 320, 384
BLOCK = 256
MESH = pl.DeviceIdType.MESH


def split(x):
    high = x.astype(bf16)
    return high, (x - high.astype(f32)).astype(bf16)


def nt(a, b):
    return lax.dot_general(a, b, (((1,), (1,)), ((), ())), preferred_element_type=f32)


def nn(a, b):
    return jnp.dot(a, b, preferred_element_type=f32)


def kernel(
    n_gx,
    n_gy,
    depth,
    rows,
    tile_ref,
    cell_ref,
    now_hbm,
    old_hbm,
    kappa_hbm,
    force_hbm,
    disp_hbm,
    vel_hbm,
    stiff_hbm,
    flag_hbm,
    next_hbm,
    before_hbm,
    disp_out,
    vel_out,
    base_out,
    soil_a,
    soil_b,
    kappa,
    force,
    disp,
    vel,
    stiff,
    flag,
    disp_new,
    vel_new,
    base,
    x_send,
    x_recv,
    x_send_top,
    x_recv_top,
    y_send,
    y_recv,
    marks,
    rank_ref,
    payload,
    recv_one,
    mid_one,
    request,
    request_t,
    hot,
    motion,
    picked,
    reply,
    recv_two,
    mid_two,
    answer,
    in_sem,
    out_sem,
    halo_send,
    halo_recv,
    one_send,
    one_recv,
    two_send,
    two_recv,
    three_send,
    three_recv,
    four_send,
    four_recv,
):
    gx, gy = lax.axis_index("gx"), lax.axis_index("gy")
    tiles = n_gx * n_gy
    count = tile_ref.shape[1]
    cells = depth * rows

    loads = []
    pairs = []
    for source, target in ((now_hbm, soil_a), (old_hbm, soil_b), (kappa_hbm, kappa)):
        for i in range(2):
            pairs.append((source.at[:, pl.ds(i * 128, 128)], target.at[i, pl.ds(PAD, cells)]))
    pairs += [
        (force_hbm, force),
        (disp_hbm, disp),
        (vel_hbm, vel),
        (stiff_hbm, stiff),
        (flag_hbm, flag),
    ]
    for i, (source, target) in enumerate(pairs):
        copy = pltpu.make_async_copy(source, target, in_sem.at[i])
        copy.start()
        loads.append(copy)

    barrier = pltpu.get_barrier_semaphore()
    for k in range(1, n_gx):
        pl.semaphore_signal(
            barrier, inc=1, device_id=(lax.rem(gx + k, n_gx), gy), device_id_type=MESH
        )
    for k in range(1, n_gy):
        pl.semaphore_signal(
            barrier, inc=1, device_id=(gx, lax.rem(gy + k, n_gy)), device_id_type=MESH
        )

    for ref in (soil_a, soil_b):
        ref[:, pl.ds(PAD + cells, rows), :] = jnp.zeros((2, rows, 128), f32)
    has = (gx > 0, gx < n_gx - 1, gy > 0, gy < n_gy - 1)
    for side in range(4):

        @pl.when(jnp.logical_not(has[side]))
        def _():
            if side < 2:
                x_recv[:, side] = jnp.zeros((STEPS, 2, depth, 128), f32)
                x_recv_top[:, side] = jnp.zeros((STEPS, 2, STEPS, 128), f32)
            else:
                y_recv[:, :, side - 2] = jnp.zeros((STEPS, 2, rows, 128), f32)

    neighbour = ((gx - 1, gy), (gx + 1, gy), (gx, gy - 1), (gx, gy + 1))

    def halo(slot, part, side, arriving=False):
        place = side if arriving else side ^ 1
        if side < 2:
            outgoing, incoming = (x_send_top, x_recv_top) if part == 0 else (x_send, x_recv)
            source, target = outgoing.at[slot, side], incoming.at[slot, place]
        else:
            source, target = y_send.at[slot, part, side - 2], y_recv.at[slot, part, place - 2]
        return pltpu.make_async_remote_copy(
            src_ref=source,
            dst_ref=target,
            send_sem=halo_send.at[slot, part, side],
            recv_sem=halo_recv.at[slot, part, place],
            device_id=neighbour[side],
            device_id_type=MESH,
        )

    def send_halo(slot, part):
        for side in range(4):

            @pl.when(has[side])
            def _():
                halo(slot, part, side).start()

    def wait_halo(slot, part):
        for side in range(4):

            @pl.when(has[side])
            def _():
                halo(slot, part, side, True).wait_recv()

    lane = lax.broadcasted_iota(jnp.int32, (rows, 128), 1)
    first_lane, last_lane = lane == 0, lane == 127
    eight = lax.broadcasted_iota(jnp.int32, (8, 128), 0)
    no_edges = (jnp.zeros((rows, 128), f32), jnp.zeros((rows, 128), f32))

    def edge_rows(slot, part, z, i, value):
        ref = x_send_top if part == 0 else x_send
        ref[slot, 0, i, pl.ds(z, 1), :] = value[0:1]
        ref[slot, 1, i, pl.ds(z, 1), :] = value[rows - 1 : rows]

    def pack(edges, z, low, high):
        here = lane == z
        return (
            jnp.where(here, jnp.broadcast_to(low[:, 0:1], (rows, 128)), edges[0]),
            jnp.where(here, jnp.broadcast_to(high[:, 127:128], (rows, 128)), edges[1]),
        )

    def keep_edges(slot, part, edges):
        y_send[slot, part, 0] = edges[0]
        y_send[slot, part, 1] = edges[1]

    def plane(z, shift=0):
        return pl.ds(PAD + z * rows + shift, rows)

    def aligned(z):
        return pl.ds(pl.multiple_of(PAD + z * rows, 8), rows)

    def advance_planes(step, out_part, in_part, here, there, layers, edges, west, east):
        incoming = x_recv_top if in_part == 0 else x_recv
        results = []
        for z, top in layers:
            fresh = []
            halves = [here[0, aligned(z), :], here[1, aligned(z), :]]
            turned = [pltpu.roll(half, 1, 1) for half in halves]
            back = [pltpu.roll(half, 127, 1) for half in halves]
            low = pltpu.roll(west, 128 - z, 1)
            high = pltpu.roll(east, 127 - z, 1)
            lows = [jnp.where(first_lane, low, turned[0]), jnp.where(first_lane, turned[0], turned[1])]
            highs = [jnp.where(last_lane, back[1], back[0]), jnp.where(last_lane, high, back[1])]
            for i in range(2):
                centre = halves[i]
                north = here[i, plane(z, -1), :]
                south = here[i, plane(z, 1), :]
                north = jnp.concatenate(
                    [jnp.where(eight == 0, incoming[step, 0, i, pl.ds(z, 1), :], north[0:8]), north[8:]],
                    0,
                )
                south = jnp.concatenate(
                    [
                        south[: rows - 8],
                        jnp.where(
                            eight == 7, incoming[step, 1, i, pl.ds(z, 1), :], south[rows - 8 :]
                        ),
                    ],
                    0,
                )
                above = centre if top else here[i, aligned(z - 1), :]
                below = here[i, aligned(z + 1), :]
                spread = (north + south) + (lows[i] + highs[i]) + (above + below) - 6.0 * centre
                value = (
                    2.0 * centre - there[i, aligned(z), :] + kappa[i, aligned(z), :] * spread
                )
                if top:
                    value = value + force_gain * force[:, i * 128 : (i + 1) * 128]
                    motion[i, pl.ds(step, rows, stride=STEPS), :] = value
                fresh.append(value)
            results.append(fresh)
        for (z, top), fresh in zip(layers, results):
            for i in range(2):
                there[i, aligned(z), :] = fresh[i]
                if step < STEPS - 1:
                    edge_rows(step + 1, out_part, z, i, fresh[i])
            edges = pack(edges, z, fresh[0], fresh[1])
        return edges

    states = (soil_a, soil_b)

    def shallow(step):
        here, there = states[step % 2], states[(step + 1) % 2]
        wait_halo(step, 0)
        west, east = y_recv[step, 0, 0], y_recv[step, 0, 1]
        edges = no_edges
        for first in range(0, STEPS - step, GROUP):
            layers = [(z, z == 0) for z in range(first, min(first + GROUP, STEPS - step))]
            edges = advance_planes(step, 0, 0, here, there, layers, edges, west, east)
        if step < STEPS - 1:
            keep_edges(step + 1, 0, edges)
            send_halo(step + 1, 0)

    def deep(step):
        here, there = states[step % 2], states[(step + 1) % 2]
        wait_halo(step, 1)
        edges, first = no_edges, STEPS - step
        if step > 0:
            edges = advance_planes(
                step, 1, 0, here, there, [(first, False)], edges, y_recv[step, 0, 0], y_recv[step, 0, 1]
            )
            first += 1
        west, east = y_recv[step, 1, 0], y_recv[step, 1, 1]
        spare = (depth - first) % GROUP
        if spare:
            layers = [(z, False) for z in range(first, first + spare)]
            edges = advance_planes(step, 1, 1, here, there, layers, edges, west, east)
            first += spare

        def some(g, kept):
            z = first + g * GROUP
            layers = [(z + i, False) for i in range(GROUP)]
            return advance_planes(step, 1, 1, here, there, layers, kept, west, east)

        edges = lax.fori_loop(0, (depth - first) // GROUP, some, edges)
        if step < STEPS - 1:
            keep_edges(step + 1, 1, edges)
            send_halo(step + 1, 1)

    for copy in loads[0:2]:
        copy.wait()

    def first_edges(part):
        def some(g, kept):
            for i in range(8):
                z = g * 8 + i
                low, high = soil_a[0, aligned(z), :], soil_a[1, aligned(z), :]
                edge_rows(0, part, z, 0, low)
                edge_rows(0, part, z, 1, high)
                kept = pack(kept, z, low, high)
            return kept

        return some

    keep_edges(0, 0, first_edges(0)(0, no_edges))
    keep_edges(0, 1, lax.fori_loop(1, depth // 8, first_edges(1), no_edges))
    pl.semaphore_wait(barrier, n_gx + n_gy - 2)
    send_halo(0, 0)
    send_halo(0, 1)

    for copy in loads[7:]:
        copy.wait()
    stiff[...] = stiff[...] * jnp.where(
        flag[...] == 0, 1.0, jnp.where(flag[...] == 1, 0.6, 0.15)
    ).astype(f32)
    payload[...] = jnp.zeros((tiles, WIDE), f32)
    before = (
        lax.broadcasted_iota(jnp.int32, (BLOCK, BLOCK), 0)
        < lax.broadcasted_iota(jnp.int32, (BLOCK, BLOCK), 1)
    ).astype(f32).astype(bf16)
    tile_number = lax.broadcasted_iota(jnp.int32, (tiles, BLOCK), 0)
    slot_number = lax.broadcasted_iota(jnp.int32, (SLOTS, BLOCK), 0)
    storey = lax.broadcasted_iota(jnp.int32, (8, BLOCK), 0)

    def list_block(j, used):
        cols = pl.ds(pl.multiple_of(j * BLOCK, BLOCK), BLOCK)
        chosen = (tile_number == tile_ref[:, cols]).astype(f32)
        mark = chosen.astype(bf16)
        marks[:, cols] = mark
        earlier = nn(mark, before) + used
        rank = jnp.sum(chosen * earlier, 0, keepdims=True).astype(jnp.int32)
        rank_ref[:, cols] = rank
        k = stiff[0:8, cols]
        of_disp = jnp.zeros((8, BLOCK), f32)
        of_vel = jnp.zeros((8, BLOCK), f32)
        coefs = jnp.zeros((8, BLOCK), f32)
        for step in reversed(range(STEPS)):
            of_vel = of_vel + of_disp
            pull = k * (jnp.where(storey == 0, 1.0, pltpu.roll(of_vel, 1, 0)) - of_vel)
            of_disp = of_disp + pull - jnp.where(storey == 7, 0.0, pltpu.roll(pull, 7, 0))
            coefs = jnp.where(storey == step, -pull[0:1], coefs)
        scale = 1.0 / STEPS
        constant = scale * jnp.sum(
            of_disp * disp[0:8, cols] + of_vel * vel[0:8, cols], 0, keepdims=True
        )
        coefs = scale * coefs
        row = (cell_ref[:, cols] // 256).astype(f32)
        col = (cell_ref[:, cols] % 256).astype(f32)
        here = slot_number == rank

        def spread_out(coef, single):
            parts = [jnp.where(rank == d, coef, 0.0) for d in range(SLOTS)]
            parts += [jnp.where(here, value, 0.0) for value in single]
            parts.append(jnp.zeros((SLOTS * (4 - len(single)), BLOCK), f32))
            return jnp.concatenate(parts, 0).astype(bf16)

        coef_high = coefs.astype(bf16).astype(f32)
        constant_high = constant.astype(bf16).astype(f32)
        payload[...] += nt(mark, spread_out(coef_high, (constant_high, row, col))) + nt(
            mark, spread_out(coefs - coef_high, (constant - constant_high,))
        )
        return used + jnp.sum(chosen, 1, keepdims=True)

    lax.fori_loop(0, count // BLOCK, list_block, jnp.zeros((tiles, 1), f32))

    def along_x(k):
        return lax.rem(gx + k, n_gx)

    def along_y(k):
        return lax.rem(gy + k, n_gy)

    def stage_x(source_of, target, send_sem, recv_sem):
        copies = []
        for k in range(1, n_gx):
            peer = along_x(k)
            copy = pltpu.make_async_remote_copy(
                src_ref=source_of(peer),
                dst_ref=target.at[gx],
                send_sem=send_sem.at[k],
                recv_sem=recv_sem.at[k],
                device_id=(peer, gy),
                device_id_type=MESH,
            )
            copy.start()
            copies.append(copy)
        return copies

    def stage_y(source_of, target, send_sem, recv_sem):
        copies = []
        for k in range(1, n_gy):
            peer = along_y(k)
            copy = pltpu.make_async_remote_copy(
                src_ref=source_of(peer),
                dst_ref=target.at[gy],
                send_sem=send_sem.at[k],
                recv_sem=recv_sem.at[k],
                device_id=(gx, peer),
                device_id_type=MESH,
            )
            copy.start()
            copies.append(copy)
        return copies

    def arrived_x(target, send_sem, recv_sem):
        for k in range(1, n_gx):
            place = target.at[lax.rem(gx + n_gx - k, n_gx)]
            pltpu.make_async_remote_copy(
                src_ref=place,
                dst_ref=place,
                send_sem=send_sem.at[k],
                recv_sem=recv_sem.at[k],
                device_id=(along_x(k), gy),
                device_id_type=MESH,
            ).wait_recv()

    def arrived_y(target, send_sem, recv_sem):
        for k in range(1, n_gy):
            place = target.at[lax.rem(gy + n_gy - k, n_gy)]
            pltpu.make_async_remote_copy(
                src_ref=place,
                dst_ref=place,
                send_sem=send_sem.at[k],
                recv_sem=recv_sem.at[k],
                device_id=(gx, along_y(k)),
                device_id_type=MESH,
            ).wait_recv()

    sends = []
    sends += stage_x(
        lambda peer: payload.at[pl.ds(pl.multiple_of(peer * n_gy, n_gy), n_gy)],
        recv_one,
        one_send,
        one_recv,
    )
    recv_one[gx] = payload[pl.ds(pl.multiple_of(gx * n_gy, n_gy), n_gy), :]

    for copy in loads[2:7]:
        copy.wait()
    shallow(0)
    deep(0)
    shallow(1)
    deep(1)

    arrived_x(recv_one, one_send, one_recv)
    for q in range(n_gy):
        for s in range(n_gx):
            mid_one[q, pl.ds(s, 1), :] = recv_one[s, pl.ds(q, 1), :]
    sends += stage_y(lambda peer: mid_one.at[peer], request, two_send, two_recv)
    request[gy] = mid_one[gy]

    shallow(2)
    deep(2)
    shallow(3)
    deep(3)

    arrived_y(request, two_send, two_recv)
    for q in range(WIDE // 128):
        request_t[pl.ds(q * 128, 128), :] = (
            request[:, :, pl.ds(q * 128, 128)].reshape(tiles, 128).T
        )
    column_number = lax.broadcasted_iota(jnp.int32, (256, 128), 0).astype(f32)

    def make_hot(d, unused):
        wanted = request_t[pl.ds(COL + d, 1), :]
        hot[:, pl.ds(pl.multiple_of(d * 128, 128), 128)] = (
            (column_number == wanted).astype(f32).astype(bf16)
        )
        return unused

    lax.fori_loop(0, SLOTS, make_hot, 0)

    for step in range(4, STEPS - 1):
        shallow(step)
        deep(step)
    shallow(STEPS - 1)

    table = jnp.concatenate(split(jnp.concatenate([motion[0], motion[1]], 1)), 1)
    line_number = lax.broadcasted_iota(jnp.int32, (rows, 128), 0).astype(f32)

    def pick(pair, unused):
        cols = pl.ds(pl.multiple_of(pair * 256, 256), 256)
        chosen = hot[:, cols]
        found = nn(table, jnp.concatenate([chosen, chosen], 0))
        for half in range(2):
            d = pair * 2 + half
            wanted = request_t[pl.ds(ROW + d, 1), :]
            total = jnp.zeros((STEPS, 128), f32)
            for r in range(rows):
                total += jnp.where(
                    wanted == float(r),
                    found[r * STEPS : (r + 1) * STEPS, half * 128 : (half + 1) * 128],
                    0.0,
                )
            picked[pl.ds(pl.multiple_of(d * STEPS, STEPS), STEPS), :] = total
        return unused

    lax.fori_loop(0, SLOTS // 2, pick, 0)
    for q in range(2):
        reply[:, :, pl.ds(q * 128, 128)] = (
            picked[pl.ds(q * 128, 128), :].T.reshape(n_gy, n_gx, 128)
        )
    sends += stage_y(lambda peer: reply.at[peer], recv_two, three_send, three_recv)
    recv_two[gy] = reply[gy]

    deep(STEPS - 1)
    stores = []
    for state, output in ((states[STEPS % 2], next_hbm), (states[(STEPS + 1) % 2], before_hbm)):
        for i in range(2):
            stores.append(
                pltpu.make_async_copy(
                    state.at[i, pl.ds(PAD, cells)],
                    output.at[:, pl.ds(i * 128, 128)],
                    out_sem.at[len(stores)],
                )
            )
            stores[-1].start()

    def land(pair, total):
        cols = pl.ds(pl.multiple_of(pair * 256, 256), 256)
        parts = []
        for half in range(2):
            d = pair * 2 + half
            eight = pl.ds(pl.multiple_of(d * STEPS, STEPS), STEPS)
            mean = request_t[pl.ds(BASE + d, 1), :] + jnp.sum(
                request_t[eight, :] * picked[eight, :], 0, keepdims=True
            )
            parts.append(jnp.where(line_number == request_t[pl.ds(ROW + d, 1), :], mean, 0.0))
        values = jnp.concatenate(parts, 1)
        return total + nt(jnp.concatenate(split(values), 0), hot[:, cols])

    landed = lax.fori_loop(0, SLOTS // 2, land, jnp.zeros((2 * rows, 256), f32))
    base[...] = landed[:rows] + landed[rows:]
    stores.append(pltpu.make_async_copy(base, base_out, out_sem.at[4]))
    stores[-1].start()

    arrived_y(recv_two, three_send, three_recv)
    for s in range(n_gx):
        for q in range(n_gy):
            mid_two[s, pl.ds(q, 1), :] = recv_two[q, pl.ds(s, 1), :]
    sends += stage_x(lambda peer: mid_two.at[peer], answer, four_send, four_recv)
    answer[gx] = mid_two[gx]
    arrived_x(answer, four_send, four_recv)

    answer_t = jnp.concatenate(
        [answer[:, :, pl.ds(q * 128, 128)].reshape(tiles, 128).T for q in range(2)], 0
    )
    decoded = jnp.concatenate(split(answer_t), 1)
    level = lax.broadcasted_iota(jnp.int32, (32, BLOCK), 0)

    def window(j, unused):
        cols = pl.ds(pl.multiple_of(j * BLOCK, BLOCK), BLOCK)
        mark = marks[:, cols]
        found = nn(decoded, jnp.concatenate([mark, mark], 0))
        rank = rank_ref[:, cols]
        ground = jnp.zeros((STEPS, BLOCK), f32)
        for d in range(SLOTS):
            ground += jnp.where(rank == d, found[d * STEPS : (d + 1) * STEPS], 0.0)
        k, place, speed = stiff[:, cols], disp[:, cols], vel[:, cols]
        for step in range(STEPS):
            beneath = jnp.where(level == 0, ground[step : step + 1], pltpu.roll(place, 1, 0))
            shear = k * (place - beneath)
            upper = jnp.where(level == 31, 0.0, pltpu.roll(shear, 31, 0))
            speed = speed + upper - shear
            place = place + speed
        disp_new[:, cols] = place
        vel_new[:, cols] = speed
        return unused

    lax.fori_loop(0, count // BLOCK, window, 0)
    stores.append(pltpu.make_async_copy(disp_new, disp_out, out_sem.at[5]))
    stores.append(pltpu.make_async_copy(vel_new, vel_out, out_sem.at[6]))
    for copy in stores[5:]:
        copy.start()
    for copy in sends:
        copy.wait_send()
    for slot in range(STEPS):
        for part in range(2):
            for side in range(4):

                @pl.when(has[side])
                def _():
                    halo(slot, part, side).wait_send()

    for copy in stores:
        copy.wait()


def shards(
    soil_now,
    soil_old,
    kappa,
    force_prev,
    storey_disp,
    storey_vel,
    stiffness,
    branch_flag,
    footprint_tile,
    footprint_cell,
):
    n_gx, n_gy = lax.axis_size("gx"), lax.axis_size("gy")
    depth, rows, wide = soil_now.shape
    storeys, count = storey_disp.shape
    tiles = n_gx * n_gy
    flat = (depth * rows, wide)
    hbm = pl.BlockSpec(memory_space=pltpu.HBM)
    dma = pltpu.SemaphoreType.DMA
    vm = pltpu.VMEM
    out = pl.pallas_call(
        functools.partial(kernel, n_gx, n_gy, depth, rows),
        out_shape=(
            jax.ShapeDtypeStruct(flat, f32),
            jax.ShapeDtypeStruct(flat, f32),
            jax.ShapeDtypeStruct((storeys, count), f32),
            jax.ShapeDtypeStruct((storeys, count), f32),
            jax.ShapeDtypeStruct((rows, wide), f32),
        ),
        in_specs=[pl.BlockSpec(memory_space=pltpu.VMEM)] * 2 + [hbm] * 8,
        out_specs=(hbm,) * 5,
        scratch_shapes=[
            vm((2, PAD + flat[0] + rows, 128), f32),
            vm((2, PAD + flat[0] + rows, 128), f32),
            vm((2, PAD + flat[0], 128), f32),
            vm((rows, wide), f32),
            vm((storeys, count), f32),
            vm((storeys, count), f32),
            vm((storeys, count), f32),
            vm((storeys, count), jnp.int32),
            vm((storeys, count), f32),
            vm((storeys, count), f32),
            vm((rows, wide), f32),
            vm((STEPS, 2, 2, depth, 128), f32),
            vm((STEPS, 2, 2, depth, 128), f32),
            vm((STEPS, 2, 2, STEPS, 128), f32),
            vm((STEPS, 2, 2, STEPS, 128), f32),
            vm((STEPS, 2, 2, rows, 128), f32),
            vm((STEPS, 2, 2, rows, 128), f32),
            vm((tiles, count), bf16),
            vm((1, count), jnp.int32),
            vm((tiles, WIDE), f32),
            vm((n_gx, n_gy, WIDE), f32),
            vm((n_gy, n_gx, WIDE), f32),
            vm((n_gy, n_gx, WIDE), f32),
            vm((WIDE, tiles), f32),
            vm((wide, SLOTS * tiles), bf16),
            vm((2, rows * STEPS, 128), f32),
            vm((SLOTS * STEPS, tiles), f32),
            vm((n_gy, n_gx, SLOTS * STEPS), f32),
            vm((n_gy, n_gx, SLOTS * STEPS), f32),
            vm((n_gx, n_gy, SLOTS * STEPS), f32),
            vm((n_gx, n_gy, SLOTS * STEPS), f32),
            dma((11,)),
            dma((7,)),
            dma((STEPS, 2, 4)),
            dma((STEPS, 2, 4)),
            dma((n_gx,)),
            dma((n_gx,)),
            dma((n_gy,)),
            dma((n_gy,)),
            dma((n_gy,)),
            dma((n_gy,)),
            dma((n_gx,)),
            dma((n_gx,)),
        ],
        compiler_params=pltpu.CompilerParams(
            collective_id=0, has_side_effects=True, vmem_limit_bytes=62 * 1024 * 1024
        ),
        cost_estimate=pl.CostEstimate(
            flops=4_000_000_000, bytes_accessed=10_000_000, transcendentals=0
        ),
    )(
        footprint_tile.reshape(1, count),
        footprint_cell.reshape(1, count),
        soil_now.reshape(flat),
        soil_old.reshape(flat),
        kappa.reshape(flat),
        force_prev,
        storey_disp,
        storey_vel,
        stiffness,
        branch_flag,
    )
    return (
        out[0].reshape(soil_now.shape),
        out[1].reshape(soil_now.shape),
        out[2],
        out[3],
        out[4],
    )


def solution(mesh):
    return jax.shard_map(
        shards,
        mesh=mesh,
        in_specs=(
            P(None, "gx", "gy"),
            P(None, "gx", "gy"),
            P(None, "gx", "gy"),
            P("gx", "gy"),
            P(None, ("gx", "gy")),
            P(None, ("gx", "gy")),
            P(None, ("gx", "gy")),
            P(None, ("gx", "gy")),
            P(("gx", "gy"), None),
            P(("gx", "gy")),
        ),
        out_specs=(
            P(None, "gx", "gy"),
            P(None, "gx", "gy"),
            P(None, ("gx", "gy")),
            P(None, ("gx", "gy")),
            P("gx", "gy"),
        ),
        check_vma=False,
    )
```

```python
import functools

import jax
import jax.numpy as jnp
from jax import lax
from jax.experimental import pallas as pl
from jax.experimental.pallas import tpu as pltpu
from jax.sharding import PartitionSpec as P

STEPS = 8
force_gain = 0.05
f32, bf16 = jnp.float32, jnp.bfloat16
GROUP = 4
PAD = 8
CHUNKS = 2
SLOTS = 32
COEF, BASE, ROW, COL, WIDE = 0, 256, 288, 320, 384
BLOCK = 256
MESH = pl.DeviceIdType.MESH


def split(x):
    high = x.astype(bf16)
    return high, (x - high.astype(f32)).astype(bf16)


def nt(a, b):
    return lax.dot_general(a, b, (((1,), (1,)), ((), ())), preferred_element_type=f32)


def nn(a, b):
    return jnp.dot(a, b, preferred_element_type=f32)


def kernel(
    n_gx,
    n_gy,
    depth,
    rows,
    tile_ref,
    cell_ref,
    now_hbm,
    old_hbm,
    kappa_hbm,
    now_deep,
    old_deep,
    kappa_deep,
    force_hbm,
    disp_hbm,
    vel_hbm,
    stiff_hbm,
    flag_hbm,
    next_hbm,
    before_hbm,
    disp_out,
    vel_out,
    base_out,
    soil_a,
    soil_b,
    kappa,
    force,
    disp,
    vel,
    stiff,
    flag,
    disp_new,
    vel_new,
    base,
    x_send,
    x_recv,
    y_send,
    y_recv,
    cone_now,
    cone_old,
    cone_kappa,
    cone_force,
    cone_send,
    cone_recv,
    marks,
    rank_ref,
    payload,
    recv_one,
    mid_one,
    request,
    request_t,
    hot,
    motion,
    picked,
    reply,
    recv_two,
    mid_two,
    answer,
    in_sem,
    out_sem,
    halo_send,
    halo_recv,
    cone_x_send,
    cone_x_recv,
    cone_y_send,
    cone_y_recv,
    one_send,
    one_recv,
    two_send,
    two_recv,
    three_send,
    three_recv,
    four_send,
    four_recv,
):
    gx, gy = lax.axis_index("gx"), lax.axis_index("gy")
    tiles = n_gx * n_gy
    count = tile_ref.shape[1]
    cells = depth * rows

    loads = []
    main = (pl.ds(STEPS, rows), pl.ds(0, 256))
    pairs = [
        (disp_hbm, disp),
        (vel_hbm, vel),
        (stiff_hbm, stiff),
        (flag_hbm, flag),
        (force_hbm, force),
        (now_deep.at[pl.ds(0, STEPS + 1)], cone_now.at[:, main[0], main[1]]),
        (old_deep.at[pl.ds(0, STEPS)], cone_old.at[:, main[0], main[1]]),
        (kappa_deep.at[pl.ds(0, STEPS)], cone_kappa.at[:, main[0], main[1]]),
        (force_hbm, cone_force.at[main[0], main[1]]),
    ]
    for source, target in ((now_hbm, soil_a), (old_hbm, soil_b), (kappa_hbm, kappa)):
        for i in range(2):
            pairs.append((source.at[:, pl.ds(i * 128, 128)], target.at[i, pl.ds(PAD, cells)]))
    for i, (source, target) in enumerate(pairs):
        copy = pltpu.make_async_copy(source, target, in_sem.at[i])
        copy.start()
        loads.append(copy)

    barrier = pltpu.get_barrier_semaphore()
    for k in range(1, n_gx):
        pl.semaphore_signal(
            barrier, inc=1, device_id=(lax.rem(gx + k, n_gx), gy), device_id_type=MESH
        )
    for k in range(1, n_gy):
        pl.semaphore_signal(
            barrier, inc=1, device_id=(gx, lax.rem(gy + k, n_gy)), device_id_type=MESH
        )

    for ref in (soil_a, soil_b):
        ref[:, pl.ds(PAD + cells, rows), :] = jnp.zeros((2, rows, 128), f32)
    has = (gx > 0, gx < n_gx - 1, gy > 0, gy < n_gy - 1)
    outside = (pl.ds(0, STEPS), pl.ds(STEPS + rows, STEPS))
    for side in range(4):

        @pl.when(jnp.logical_not(has[side]))
        def _():
            if side < 2:
                x_recv[:, side] = jnp.zeros((STEPS, 2, depth, 128), f32)
                for ref in (cone_now, cone_old, cone_kappa):
                    ref[:, outside[side], pl.ds(0, 256)] = jnp.zeros(
                        (ref.shape[0], STEPS, 256), f32
                    )
                cone_force[outside[side], pl.ds(0, 256)] = jnp.zeros((STEPS, 256), f32)
            else:
                y_recv[:, :, side - 2] = jnp.zeros((STEPS, CHUNKS, rows, 128), f32)
                cone_recv[side - 2] = jnp.zeros(cone_recv.shape[1:], f32)

    neighbour = ((gx - 1, gy), (gx + 1, gy), (gx, gy - 1), (gx, gy + 1))

    def cone_x(side, arriving=False):
        copies = []
        sources = (
            now_deep.at[pl.ds(0, STEPS + 1)],
            old_deep.at[pl.ds(0, STEPS)],
            kappa_deep.at[pl.ds(0, STEPS)],
        )
        edge = pl.ds(0, STEPS) if side == 0 else pl.ds(rows - STEPS, STEPS)
        place = side if arriving else side ^ 1
        for i, target in enumerate((cone_now, cone_old, cone_kappa, cone_force)):
            if i < 3:
                source = sources[i].at[:, edge, :]
                target = target.at[:, outside[place], pl.ds(0, 256)]
            else:
                source = force_hbm.at[edge, :]
                target = target.at[outside[place], pl.ds(0, 256)]
            copies.append(
                pltpu.make_async_remote_copy(
                    src_ref=source,
                    dst_ref=target,
                    send_sem=cone_x_send.at[i, side],
                    recv_sem=cone_x_recv.at[i, place],
                    device_id=neighbour[side],
                    device_id_type=MESH,
                )
            )
        return copies

    def cone_y(side, arriving=False):
        place = side if arriving else side ^ 1
        return pltpu.make_async_remote_copy(
            src_ref=cone_send.at[side],
            dst_ref=cone_recv.at[place],
            send_sem=cone_y_send.at[side],
            recv_sem=cone_y_recv.at[place],
            device_id=neighbour[2 + side],
            device_id_type=MESH,
        )

    around = rows + 2 * STEPS
    cone_lane = lax.broadcasted_iota(jnp.int32, (around, 128), 1)
    each = [(cone_now, z) for z in range(STEPS + 1)]
    each += [(ref, z) for ref in (cone_old, cone_kappa) for z in range(STEPS)]
    each += [(cone_force, None)]
    width = 128 // STEPS

    def cone_layer(ref, z, cols):
        return ref[:, cols] if z is None else ref[z, :, cols]

    def cone_edges():
        for group in range(2):
            west = jnp.zeros((around, 128), f32)
            east = jnp.zeros((around, 128), f32)
            for slot, (ref, z) in enumerate(each[group * width : (group + 1) * width]):
                here = (cone_lane // STEPS) == slot
                low = cone_layer(ref, z, pl.ds(0, 128))
                high = cone_layer(ref, z, pl.ds(128, 128))
                low = pltpu.roll(low, slot * STEPS, 1) if slot else low
                west = jnp.where(here, low, west)
                high = pltpu.roll(high, (slot + 1) * STEPS, 1) if slot < width - 1 else high
                east = jnp.where(here, high, east)
            cone_send[0, group] = west
            cone_send[1, group] = east

    def cone_sides():
        for group in range(2):
            west, east = cone_recv[0, group], cone_recv[1, group]
            for slot, (ref, z) in enumerate(each[group * width : (group + 1) * width]):
                low = pltpu.roll(west, 128 - (slot + 1) * STEPS, 1) if slot < width - 1 else west
                high = pltpu.roll(east, 128 - slot * STEPS, 1) if slot else east
                value = jnp.where(
                    cone_lane >= 128 - STEPS, low, jnp.where(cone_lane < STEPS, high, 0.0)
                )
                if z is None:
                    ref[:, pl.ds(256, 128)] = value
                else:
                    ref[z, :, pl.ds(256, 128)] = value

    def cone_steps():
        for step in range(STEPS):
            here, there = (cone_now, cone_old) if step % 2 == 0 else (cone_old, cone_now)
            for z in range(STEPS - step):
                centre = here[z]
                above = centre if z == 0 else here[z - 1]
                spread = (
                    (pltpu.roll(centre, 1, 0) + pltpu.roll(centre, around - 1, 0))
                    + (pltpu.roll(centre, 1, 1) + pltpu.roll(centre, 383, 1))
                    + (above + here[z + 1])
                    - 6.0 * centre
                )
                value = 2.0 * centre - there[z] + cone_kappa[z] * spread
                if z == 0:
                    value = value + force_gain * cone_force[...]
                    for i in range(2):
                        motion[i, pl.ds(step, rows, stride=STEPS), :] = value[
                            STEPS : STEPS + rows, i * 128 : (i + 1) * 128
                        ]
                there[z] = value

    planes = depth // CHUNKS

    def halo(slot, part, side, arriving=False):
        place = side if arriving else side ^ 1
        if side < 2:
            layers = pl.ds(part * planes, planes)
            source = x_send.at[slot, side, :, layers]
            target = x_recv.at[slot, place, :, layers]
        else:
            source, target = y_send.at[slot, part], y_recv.at[slot, part, place - 2]
        return pltpu.make_async_remote_copy(
            src_ref=source,
            dst_ref=target,
            send_sem=halo_send.at[slot, part, side],
            recv_sem=halo_recv.at[slot, part, place],
            device_id=neighbour[side],
            device_id_type=MESH,
        )

    def send_halo(slot, part):
        for side in range(4):

            @pl.when(has[side])
            def _():
                halo(slot, part, side).start()

    def wait_halo(slot, part):
        for side in range(4):

            @pl.when(has[side])
            def _():
                halo(slot, part, side, True).wait_recv()

    lane = lax.broadcasted_iota(jnp.int32, (rows, 128), 1)
    first_lane, last_lane = lane == 0, lane == 127
    odd_lane = (lane % 2) == 1
    pair_of = lane // 2
    eight = lax.broadcasted_iota(jnp.int32, (8, 128), 0)
    no_edges = jnp.zeros((rows, 128), f32)

    def edge_rows(slot, z, i, value):
        x_send[slot, 0, i, pl.ds(z, 1), :] = value[0:1]
        x_send[slot, 1, i, pl.ds(z, 1), :] = value[rows - 1 : rows]

    def pack(edges, z, low, high):
        both = pltpu.roll(jnp.where(first_lane, low, high), 2 * z + 1, 1)
        return jnp.where(pair_of == z, both, edges)

    def plane(z, shift=0):
        return pl.ds(PAD + z * rows + shift, rows)

    def aligned(z):
        return pl.ds(pl.multiple_of(PAD + z * rows, 8), rows)

    def advance_planes(step, here, there, layers, edges, sides):
        results = []
        for z, top in layers:
            fresh = []
            halves = [here[0, aligned(z), :], here[1, aligned(z), :]]
            turned = [pltpu.roll(half, 1, 1) for half in halves]
            back = [pltpu.roll(half, 127, 1) for half in halves]
            beside = pltpu.roll(sides, 127 - 2 * z, 1)
            lows = [
                jnp.where(first_lane, beside, turned[0]),
                jnp.where(first_lane, turned[0], turned[1]),
            ]
            highs = [
                jnp.where(last_lane, back[1], back[0]),
                jnp.where(last_lane, beside, back[1]),
            ]
            for i in range(2):
                centre = halves[i]
                north = here[i, plane(z, -1), :]
                south = here[i, plane(z, 1), :]
                edge = jnp.where(eight == 0, x_recv[step, 0, i, pl.ds(z, 1), :], north[0:8])
                north = jnp.concatenate([edge, north[8:]], 0)
                edge = jnp.where(
                    eight == 7, x_recv[step, 1, i, pl.ds(z, 1), :], south[rows - 8 :]
                )
                south = jnp.concatenate([south[: rows - 8], edge], 0)
                above = centre if top else here[i, aligned(z - 1), :]
                below = here[i, aligned(z + 1), :]
                spread = (north + south) + (lows[i] + highs[i]) + (above + below) - 6.0 * centre
                value = (
                    2.0 * centre - there[i, aligned(z), :] + kappa[i, aligned(z), :] * spread
                )
                if top:
                    value = value + force_gain * force[:, i * 128 : (i + 1) * 128]
                fresh.append(value)
            results.append(fresh)
        for (z, top), fresh in zip(layers, results):
            for i in range(2):
                there[i, aligned(z), :] = fresh[i]
                if step < STEPS - 1:
                    edge_rows(step + 1, z, i, fresh[i])
            if step < STEPS - 1:
                edges = pack(edges, z, fresh[0], fresh[1])
        return edges

    states = (soil_a, soil_b)

    def advance(step, part):
        here, there = states[step % 2], states[(step + 1) % 2]
        wait_halo(step, part)
        first, last = part * planes, (part + 1) * planes
        sides = jnp.where(
            odd_lane,
            pltpu.roll(y_recv[step, part, 0], 1, 1),
            pltpu.roll(y_recv[step, part, 1], 127, 1),
        )
        edges = no_edges
        if part == 0:
            layers = [(z, z == 0) for z in range(GROUP)]
            edges = advance_planes(step, here, there, layers, edges, sides)
            first = GROUP

        def some(g, kept):
            z = first + g * GROUP
            layers = [(z + i, False) for i in range(GROUP)]
            return advance_planes(step, here, there, layers, kept, sides)

        edges = lax.fori_loop(0, (last - first) // GROUP, some, edges)
        if step < STEPS - 1:
            y_send[step + 1, part] = edges
            send_halo(step + 1, part)

    def soil_step(step):
        for part in range(CHUNKS):
            advance(step, part)

    pl.semaphore_wait(barrier, n_gx + n_gy - 2)
    for side in range(2):

        @pl.when(has[side])
        def _():
            for copy in cone_x(side):
                copy.start()

    for copy in loads[9:11]:
        copy.wait()
    for part in range(CHUNKS):

        def first_edges(g, kept):
            for i in range(8):
                z = part * planes + g * 8 + i
                low, high = soil_a[0, aligned(z), :], soil_a[1, aligned(z), :]
                edge_rows(0, z, 0, low)
                edge_rows(0, z, 1, high)
                kept = pack(kept, z, low, high)
            return kept

        y_send[0, part] = lax.fori_loop(0, planes // 8, first_edges, no_edges)
        send_halo(0, part)

    for copy in loads[0:4]:
        copy.wait()
    stiff[...] = stiff[...] * jnp.where(
        flag[...] == 0, 1.0, jnp.where(flag[...] == 1, 0.6, 0.15)
    ).astype(f32)
    payload[...] = jnp.zeros((tiles, WIDE), f32)
    before = (
        lax.broadcasted_iota(jnp.int32, (BLOCK, BLOCK), 0)
        < lax.broadcasted_iota(jnp.int32, (BLOCK, BLOCK), 1)
    ).astype(f32).astype(bf16)
    tile_number = lax.broadcasted_iota(jnp.int32, (tiles, BLOCK), 0)
    slot_number = lax.broadcasted_iota(jnp.int32, (SLOTS, BLOCK), 0)
    storey = lax.broadcasted_iota(jnp.int32, (8, BLOCK), 0)

    def list_block(j, used):
        cols = pl.ds(pl.multiple_of(j * BLOCK, BLOCK), BLOCK)
        chosen = (tile_number == tile_ref[:, cols]).astype(f32)
        mark = chosen.astype(bf16)
        marks[:, cols] = mark
        earlier = nn(mark, before) + used
        rank = jnp.sum(chosen * earlier, 0, keepdims=True).astype(jnp.int32)
        rank_ref[:, cols] = rank
        k = stiff[0:8, cols]
        of_disp = jnp.zeros((8, BLOCK), f32)
        of_vel = jnp.zeros((8, BLOCK), f32)
        coefs = jnp.zeros((8, BLOCK), f32)
        for step in reversed(range(STEPS)):
            of_vel = of_vel + of_disp
            pull = k * (jnp.where(storey == 0, 1.0, pltpu.roll(of_vel, 1, 0)) - of_vel)
            of_disp = of_disp + pull - jnp.where(storey == 7, 0.0, pltpu.roll(pull, 7, 0))
            coefs = jnp.where(storey == step, -pull[0:1], coefs)
        scale = 1.0 / STEPS
        constant = scale * jnp.sum(
            of_disp * disp[0:8, cols] + of_vel * vel[0:8, cols], 0, keepdims=True
        )
        coefs = scale * coefs
        row = (cell_ref[:, cols] // 256).astype(f32)
        col = (cell_ref[:, cols] % 256).astype(f32)
        here = slot_number == rank

        def spread_out(coef, single):
            parts = [jnp.where(rank == d, coef, 0.0) for d in range(SLOTS)]
            parts += [jnp.where(here, value, 0.0) for value in single]
            parts.append(jnp.zeros((SLOTS * (4 - len(single)), BLOCK), f32))
            return jnp.concatenate(parts, 0).astype(bf16)

        coef_high = coefs.astype(bf16).astype(f32)
        constant_high = constant.astype(bf16).astype(f32)
        payload[...] += nt(mark, spread_out(coef_high, (constant_high, row, col))) + nt(
            mark, spread_out(coefs - coef_high, (constant - constant_high,))
        )
        return used + jnp.sum(chosen, 1, keepdims=True)

    lax.fori_loop(0, count // BLOCK, list_block, jnp.zeros((tiles, 1), f32))

    def along_x(k):
        return lax.rem(gx + k, n_gx)

    def along_y(k):
        return lax.rem(gy + k, n_gy)

    def stage_x(source_of, target, send_sem, recv_sem):
        copies = []
        for k in range(1, n_gx):
            peer = along_x(k)
            copy = pltpu.make_async_remote_copy(
                src_ref=source_of(peer),
                dst_ref=target.at[gx],
                send_sem=send_sem.at[k],
                recv_sem=recv_sem.at[k],
                device_id=(peer, gy),
                device_id_type=MESH,
            )
            copy.start()
            copies.append(copy)
        return copies

    def stage_y(source_of, target, send_sem, recv_sem):
        copies = []
        for k in range(1, n_gy):
            peer = along_y(k)
            copy = pltpu.make_async_remote_copy(
                src_ref=source_of(peer),
                dst_ref=target.at[gy],
                send_sem=send_sem.at[k],
                recv_sem=recv_sem.at[k],
                device_id=(gx, peer),
                device_id_type=MESH,
            )
            copy.start()
            copies.append(copy)
        return copies

    def arrived_x(target, send_sem, recv_sem):
        for k in range(1, n_gx):
            place = target.at[lax.rem(gx + n_gx - k, n_gx)]
            pltpu.make_async_remote_copy(
                src_ref=place,
                dst_ref=place,
                send_sem=send_sem.at[k],
                recv_sem=recv_sem.at[k],
                device_id=(along_x(k), gy),
                device_id_type=MESH,
            ).wait_recv()

    def arrived_y(target, send_sem, recv_sem):
        for k in range(1, n_gy):
            place = target.at[lax.rem(gy + n_gy - k, n_gy)]
            pltpu.make_async_remote_copy(
                src_ref=place,
                dst_ref=place,
                send_sem=send_sem.at[k],
                recv_sem=recv_sem.at[k],
                device_id=(gx, along_y(k)),
                device_id_type=MESH,
            ).wait_recv()

    sends = []
    sends += stage_x(
        lambda peer: payload.at[pl.ds(pl.multiple_of(peer * n_gy, n_gy), n_gy)],
        recv_one,
        one_send,
        one_recv,
    )
    recv_one[gx] = payload[pl.ds(pl.multiple_of(gx * n_gy, n_gy), n_gy), :]

    for copy in loads[4:9]:
        copy.wait()
    for side in range(2):

        @pl.when(has[side])
        def _():
            for copy in cone_x(side, True):
                copy.wait_recv()

    cone_edges()
    for side in range(2):

        @pl.when(has[2 + side])
        def _():
            cone_y(side).start()

    for copy in loads[11:]:
        copy.wait()
    soil_step(0)
    for side in range(2):

        @pl.when(has[2 + side])
        def _():
            cone_y(side, True).wait_recv()

    cone_sides()
    cone_steps()

    arrived_x(recv_one, one_send, one_recv)
    for q in range(n_gy):
        for s in range(n_gx):
            mid_one[q, pl.ds(s, 1), :] = recv_one[s, pl.ds(q, 1), :]
    sends += stage_y(lambda peer: mid_one.at[peer], request, two_send, two_recv)
    request[gy] = mid_one[gy]

    soil_step(1)
    soil_step(2)

    arrived_y(request, two_send, two_recv)
    for q in range(WIDE // 128):
        request_t[pl.ds(q * 128, 128), :] = (
            request[:, :, pl.ds(q * 128, 128)].reshape(tiles, 128).T
        )
    column_number = lax.broadcasted_iota(jnp.int32, (256, 128), 0).astype(f32)

    def make_hot(d, unused):
        wanted = request_t[pl.ds(COL + d, 1), :]
        hot[:, pl.ds(pl.multiple_of(d * 128, 128), 128)] = (
            (column_number == wanted).astype(f32).astype(bf16)
        )
        return unused

    lax.fori_loop(0, SLOTS, make_hot, 0)

    table = jnp.concatenate(split(jnp.concatenate([motion[0], motion[1]], 1)), 1)
    line_number = lax.broadcasted_iota(jnp.int32, (rows, 128), 0).astype(f32)

    def pick(pair, unused):
        cols = pl.ds(pl.multiple_of(pair * 256, 256), 256)
        chosen = hot[:, cols]
        found = nn(table, jnp.concatenate([chosen, chosen], 0))
        for half in range(2):
            d = pair * 2 + half
            wanted = request_t[pl.ds(ROW + d, 1), :]
            total = jnp.zeros((STEPS, 128), f32)
            for r in range(rows):
                total += jnp.where(
                    wanted == float(r),
                    found[r * STEPS : (r + 1) * STEPS, half * 128 : (half + 1) * 128],
                    0.0,
                )
            picked[pl.ds(pl.multiple_of(d * STEPS, STEPS), STEPS), :] = total
        return unused

    lax.fori_loop(0, SLOTS // 2, pick, 0)
    for q in range(2):
        reply[:, :, pl.ds(q * 128, 128)] = (
            picked[pl.ds(q * 128, 128), :].T.reshape(n_gy, n_gx, 128)
        )
    sends += stage_y(lambda peer: reply.at[peer], recv_two, three_send, three_recv)
    recv_two[gy] = reply[gy]

    stores = []
    soil_step(3)

    def land(pair, total):
        cols = pl.ds(pl.multiple_of(pair * 256, 256), 256)
        parts = []
        for half in range(2):
            d = pair * 2 + half
            eight = pl.ds(pl.multiple_of(d * STEPS, STEPS), STEPS)
            mean = request_t[pl.ds(BASE + d, 1), :] + jnp.sum(
                request_t[eight, :] * picked[eight, :], 0, keepdims=True
            )
            parts.append(jnp.where(line_number == request_t[pl.ds(ROW + d, 1), :], mean, 0.0))
        values = jnp.concatenate(parts, 1)
        return total + nt(jnp.concatenate(split(values), 0), hot[:, cols])

    landed = lax.fori_loop(0, SLOTS // 2, land, jnp.zeros((2 * rows, 256), f32))
    base[...] = landed[:rows] + landed[rows:]
    stores.append(pltpu.make_async_copy(base, base_out, out_sem.at[0]))
    stores[-1].start()

    soil_step(4)
    arrived_y(recv_two, three_send, three_recv)
    for s in range(n_gx):
        for q in range(n_gy):
            mid_two[s, pl.ds(q, 1), :] = recv_two[q, pl.ds(s, 1), :]
    sends += stage_x(lambda peer: mid_two.at[peer], answer, four_send, four_recv)
    answer[gx] = mid_two[gx]
    soil_step(5)
    soil_step(6)
    arrived_x(answer, four_send, four_recv)

    answer_t = jnp.concatenate(
        [answer[:, :, pl.ds(q * 128, 128)].reshape(tiles, 128).T for q in range(2)], 0
    )
    decoded = jnp.concatenate(split(answer_t), 1)
    level = lax.broadcasted_iota(jnp.int32, (32, BLOCK), 0)

    def window(j, unused):
        cols = pl.ds(pl.multiple_of(j * BLOCK, BLOCK), BLOCK)
        mark = marks[:, cols]
        found = nn(decoded, jnp.concatenate([mark, mark], 0))
        rank = rank_ref[:, cols]
        ground = jnp.zeros((STEPS, BLOCK), f32)
        for d in range(SLOTS):
            ground += jnp.where(rank == d, found[d * STEPS : (d + 1) * STEPS], 0.0)
        k, place, speed = stiff[:, cols], disp[:, cols], vel[:, cols]
        for step in range(STEPS):
            beneath = jnp.where(level == 0, ground[step : step + 1], pltpu.roll(place, 1, 0))
            shear = k * (place - beneath)
            upper = jnp.where(level == 31, 0.0, pltpu.roll(shear, 31, 0))
            speed = speed + upper - shear
            place = place + speed
        disp_new[:, cols] = place
        vel_new[:, cols] = speed
        return unused

    lax.fori_loop(0, count // BLOCK, window, 0)
    stores.append(pltpu.make_async_copy(disp_new, disp_out, out_sem.at[1]))
    stores.append(pltpu.make_async_copy(vel_new, vel_out, out_sem.at[2]))
    for copy in stores[1:]:
        copy.start()

    soil_step(7)
    for state, output in ((states[STEPS % 2], next_hbm), (states[(STEPS + 1) % 2], before_hbm)):
        for i in range(2):
            stores.append(
                pltpu.make_async_copy(
                    state.at[i, pl.ds(PAD, cells)],
                    output.at[:, pl.ds(i * 128, 128)],
                    out_sem.at[len(stores)],
                )
            )
            stores[-1].start()
    for side in range(2):

        @pl.when(has[side])
        def _():
            for copy in cone_x(side):
                copy.wait_send()

        @pl.when(has[2 + side])
        def _():
            cone_y(side).wait_send()

    for copy in sends:
        copy.wait_send()
    for slot in range(STEPS):
        for part in range(CHUNKS):
            for side in range(4):

                @pl.when(has[side])
                def _():
                    halo(slot, part, side).wait_send()

    for copy in stores:
        copy.wait()


def shards(
    soil_now,
    soil_old,
    kappa,
    force_prev,
    storey_disp,
    storey_vel,
    stiffness,
    branch_flag,
    footprint_tile,
    footprint_cell,
):
    n_gx, n_gy = lax.axis_size("gx"), lax.axis_size("gy")
    depth, rows, wide = soil_now.shape
    storeys, count = storey_disp.shape
    tiles = n_gx * n_gy
    flat = (depth * rows, wide)
    around = rows + 2 * STEPS
    hbm = pl.BlockSpec(memory_space=pltpu.HBM)
    dma = pltpu.SemaphoreType.DMA
    vm = pltpu.VMEM
    out = pl.pallas_call(
        functools.partial(kernel, n_gx, n_gy, depth, rows),
        out_shape=(
            jax.ShapeDtypeStruct(flat, f32),
            jax.ShapeDtypeStruct(flat, f32),
            jax.ShapeDtypeStruct((storeys, count), f32),
            jax.ShapeDtypeStruct((storeys, count), f32),
            jax.ShapeDtypeStruct((rows, wide), f32),
        ),
        in_specs=[pl.BlockSpec(memory_space=pltpu.VMEM)] * 2 + [hbm] * 11,
        out_specs=(hbm,) * 5,
        scratch_shapes=[
            vm((2, PAD + flat[0] + rows, 128), f32),
            vm((2, PAD + flat[0] + rows, 128), f32),
            vm((2, PAD + flat[0], 128), f32),
            vm((rows, wide), f32),
            vm((storeys, count), f32),
            vm((storeys, count), f32),
            vm((storeys, count), f32),
            vm((storeys, count), jnp.int32),
            vm((storeys, count), f32),
            vm((storeys, count), f32),
            vm((rows, wide), f32),
            vm((STEPS, 2, 2, depth, 128), f32),
            vm((STEPS, 2, 2, depth, 128), f32),
            vm((STEPS, CHUNKS, rows, 128), f32),
            vm((STEPS, CHUNKS, 2, rows, 128), f32),
            vm((STEPS + 1, around, 384), f32),
            vm((STEPS, around, 384), f32),
            vm((STEPS, around, 384), f32),
            vm((around, 384), f32),
            vm((2, 2, around, 128), f32),
            vm((2, 2, around, 128), f32),
            vm((tiles, count), bf16),
            vm((1, count), jnp.int32),
            vm((tiles, WIDE), f32),
            vm((n_gx, n_gy, WIDE), f32),
            vm((n_gy, n_gx, WIDE), f32),
            vm((n_gy, n_gx, WIDE), f32),
            vm((WIDE, tiles), f32),
            vm((wide, SLOTS * tiles), bf16),
            vm((2, rows * STEPS, 128), f32),
            vm((SLOTS * STEPS, tiles), f32),
            vm((n_gy, n_gx, SLOTS * STEPS), f32),
            vm((n_gy, n_gx, SLOTS * STEPS), f32),
            vm((n_gx, n_gy, SLOTS * STEPS), f32),
            vm((n_gx, n_gy, SLOTS * STEPS), f32),
            dma((15,)),
            dma((7,)),
            dma((STEPS, CHUNKS, 4)),
            dma((STEPS, CHUNKS, 4)),
            dma((4, 2)),
            dma((4, 2)),
            dma((2,)),
            dma((2,)),
            dma((n_gx,)),
            dma((n_gx,)),
            dma((n_gy,)),
            dma((n_gy,)),
            dma((n_gy,)),
            dma((n_gy,)),
            dma((n_gx,)),
            dma((n_gx,)),
        ],
        compiler_params=pltpu.CompilerParams(
            collective_id=0, has_side_effects=True, vmem_limit_bytes=62 * 1024 * 1024
        ),
        cost_estimate=pl.CostEstimate(
            flops=4_000_000_000, bytes_accessed=10_000_000, transcendentals=0
        ),
    )(
        footprint_tile.reshape(1, count),
        footprint_cell.reshape(1, count),
        soil_now.reshape(flat),
        soil_old.reshape(flat),
        kappa.reshape(flat),
        soil_now,
        soil_old,
        kappa,
        force_prev,
        storey_disp,
        storey_vel,
        stiffness,
        branch_flag,
    )
    return (
        out[0].reshape(soil_now.shape),
        out[1].reshape(soil_now.shape),
        out[2],
        out[3],
        out[4],
    )


def solution(mesh):
    return jax.shard_map(
        shards,
        mesh=mesh,
        in_specs=(
            P(None, "gx", "gy"),
            P(None, "gx", "gy"),
            P(None, "gx", "gy"),
            P("gx", "gy"),
            P(None, ("gx", "gy")),
            P(None, ("gx", "gy")),
            P(None, ("gx", "gy")),
            P(None, ("gx", "gy")),
            P(("gx", "gy"), None),
            P(("gx", "gy")),
        ),
        out_specs=(
            P(None, "gx", "gy"),
            P(None, "gx", "gy"),
            P(None, ("gx", "gy")),
            P(None, ("gx", "gy")),
            P("gx", "gy"),
        ),
        check_vma=False,
    )
```

```python
import functools

import jax
import jax.numpy as jnp
from jax import lax
from jax.experimental import pallas as pl
from jax.experimental.pallas import tpu as pltpu
from jax.sharding import PartitionSpec as P

STEPS = 8
force_gain = 0.05
f32, bf16 = jnp.float32, jnp.bfloat16
GROUP = 8
PAD = 8
CHUNKS = 2
SLOTS = 32
COEF, BASE, ROW, COL, WIDE = 0, 256, 288, 320, 384
BLOCK = 256
MESH = pl.DeviceIdType.MESH


def split(x):
    high = x.astype(bf16)
    return high, (x - high.astype(f32)).astype(bf16)


def nt(a, b):
    return lax.dot_general(a, b, (((1,), (1,)), ((), ())), preferred_element_type=f32)


def nn(a, b):
    return jnp.dot(a, b, preferred_element_type=f32)


def kernel(
    n_gx,
    n_gy,
    depth,
    rows,
    tile_ref,
    cell_ref,
    now_hbm,
    old_hbm,
    kappa_hbm,
    now_deep,
    old_deep,
    kappa_deep,
    force_hbm,
    disp_hbm,
    vel_hbm,
    stiff_hbm,
    flag_hbm,
    next_hbm,
    before_hbm,
    disp_out,
    vel_out,
    base_out,
    soil_a,
    soil_b,
    kappa,
    force,
    disp,
    vel,
    stiff,
    flag,
    disp_new,
    vel_new,
    base,
    x_send,
    x_recv,
    y_send,
    y_recv,
    cone_now,
    cone_old,
    cone_kappa,
    cone_force,
    cone_send,
    cone_recv,
    marks,
    rank_ref,
    payload,
    recv_one,
    mid_one,
    request,
    request_t,
    hot,
    motion,
    picked,
    reply,
    recv_two,
    mid_two,
    answer,
    in_sem,
    out_sem,
    halo_send,
    halo_recv,
    cone_x_send,
    cone_x_recv,
    cone_y_send,
    cone_y_recv,
    one_send,
    one_recv,
    two_send,
    two_recv,
    three_send,
    three_recv,
    four_send,
    four_recv,
):
    gx, gy = lax.axis_index("gx"), lax.axis_index("gy")
    tiles = n_gx * n_gy
    count = tile_ref.shape[1]
    cells = depth * rows

    loads = []
    main = (pl.ds(STEPS, rows), pl.ds(0, 256))
    pairs = [
        (disp_hbm, disp),
        (vel_hbm, vel),
        (stiff_hbm, stiff),
        (flag_hbm, flag),
        (force_hbm, force),
        (now_deep.at[pl.ds(0, STEPS + 1)], cone_now.at[:, main[0], main[1]]),
        (old_deep.at[pl.ds(0, STEPS)], cone_old.at[:, main[0], main[1]]),
        (kappa_deep.at[pl.ds(0, STEPS)], cone_kappa.at[:, main[0], main[1]]),
        (force_hbm, cone_force.at[main[0], main[1]]),
    ]
    for source, target in ((now_hbm, soil_a), (old_hbm, soil_b), (kappa_hbm, kappa)):
        for i in range(2):
            pairs.append((source.at[:, pl.ds(i * 128, 128)], target.at[i, pl.ds(PAD, cells)]))
    for i, (source, target) in enumerate(pairs):
        copy = pltpu.make_async_copy(source, target, in_sem.at[i])
        copy.start()
        loads.append(copy)

    barrier = pltpu.get_barrier_semaphore()
    for k in range(1, n_gx):
        pl.semaphore_signal(
            barrier, inc=1, device_id=(lax.rem(gx + k, n_gx), gy), device_id_type=MESH
        )
    for k in range(1, n_gy):
        pl.semaphore_signal(
            barrier, inc=1, device_id=(gx, lax.rem(gy + k, n_gy)), device_id_type=MESH
        )

    for ref in (soil_a, soil_b):
        ref[:, pl.ds(PAD + cells, rows), :] = jnp.zeros((2, rows, 128), f32)
    has = (gx > 0, gx < n_gx - 1, gy > 0, gy < n_gy - 1)
    outside = (pl.ds(0, STEPS), pl.ds(STEPS + rows, STEPS))
    for side in range(4):

        @pl.when(jnp.logical_not(has[side]))
        def _():
            if side < 2:
                x_recv[:, side] = jnp.zeros((STEPS, 2, depth, 128), f32)
                for ref in (cone_now, cone_old, cone_kappa):
                    ref[:, outside[side], pl.ds(0, 256)] = jnp.zeros(
                        (ref.shape[0], STEPS, 256), f32
                    )
                cone_force[outside[side], pl.ds(0, 256)] = jnp.zeros((STEPS, 256), f32)
            else:
                y_recv[:, :, side - 2] = jnp.zeros((STEPS, CHUNKS, rows, 128), f32)
                cone_recv[side - 2] = jnp.zeros(cone_recv.shape[1:], f32)

    neighbour = ((gx - 1, gy), (gx + 1, gy), (gx, gy - 1), (gx, gy + 1))

    def cone_x(side, arriving=False):
        copies = []
        sources = (
            now_deep.at[pl.ds(0, STEPS + 1)],
            old_deep.at[pl.ds(0, STEPS)],
            kappa_deep.at[pl.ds(0, STEPS)],
        )
        edge = pl.ds(0, STEPS) if side == 0 else pl.ds(rows - STEPS, STEPS)
        place = side if arriving else side ^ 1
        for i, target in enumerate((cone_now, cone_old, cone_kappa, cone_force)):
            if i < 3:
                source = sources[i].at[:, edge, :]
                target = target.at[:, outside[place], pl.ds(0, 256)]
            else:
                source = force_hbm.at[edge, :]
                target = target.at[outside[place], pl.ds(0, 256)]
            copies.append(
                pltpu.make_async_remote_copy(
                    src_ref=source,
                    dst_ref=target,
                    send_sem=cone_x_send.at[i, side],
                    recv_sem=cone_x_recv.at[i, place],
                    device_id=neighbour[side],
                    device_id_type=MESH,
                )
            )
        return copies

    def cone_y(side, arriving=False):
        place = side if arriving else side ^ 1
        return pltpu.make_async_remote_copy(
            src_ref=cone_send.at[side],
            dst_ref=cone_recv.at[place],
            send_sem=cone_y_send.at[side],
            recv_sem=cone_y_recv.at[place],
            device_id=neighbour[2 + side],
            device_id_type=MESH,
        )

    around = rows + 2 * STEPS
    cone_lane = lax.broadcasted_iota(jnp.int32, (around, 128), 1)
    each = [(cone_now, z) for z in range(STEPS + 1)]
    each += [(ref, z) for ref in (cone_old, cone_kappa) for z in range(STEPS)]
    each += [(cone_force, None)]
    width = 128 // STEPS

    def cone_layer(ref, z, cols):
        return ref[:, cols] if z is None else ref[z, :, cols]

    def cone_edges():
        for group in range(2):
            west = jnp.zeros((around, 128), f32)
            east = jnp.zeros((around, 128), f32)
            for slot, (ref, z) in enumerate(each[group * width : (group + 1) * width]):
                here = (cone_lane // STEPS) == slot
                low = cone_layer(ref, z, pl.ds(0, 128))
                high = cone_layer(ref, z, pl.ds(128, 128))
                low = pltpu.roll(low, slot * STEPS, 1) if slot else low
                west = jnp.where(here, low, west)
                high = pltpu.roll(high, (slot + 1) * STEPS, 1) if slot < width - 1 else high
                east = jnp.where(here, high, east)
            cone_send[0, group] = west
            cone_send[1, group] = east

    def cone_sides():
        for group in range(2):
            west, east = cone_recv[0, group], cone_recv[1, group]
            for slot, (ref, z) in enumerate(each[group * width : (group + 1) * width]):
                low = pltpu.roll(west, 128 - (slot + 1) * STEPS, 1) if slot < width - 1 else west
                high = pltpu.roll(east, 128 - slot * STEPS, 1) if slot else east
                value = jnp.where(
                    cone_lane >= 128 - STEPS, low, jnp.where(cone_lane < STEPS, high, 0.0)
                )
                if z is None:
                    ref[:, pl.ds(256, 128)] = value
                else:
                    ref[z, :, pl.ds(256, 128)] = value

    def cone_steps():
        for step in range(STEPS):
            here, there = (cone_now, cone_old) if step % 2 == 0 else (cone_old, cone_now)
            for z in range(STEPS - step):
                centre = here[z]
                above = centre if z == 0 else here[z - 1]
                spread = (
                    (pltpu.roll(centre, 1, 0) + pltpu.roll(centre, around - 1, 0))
                    + (pltpu.roll(centre, 1, 1) + pltpu.roll(centre, 383, 1))
                    + (above + here[z + 1])
                    - 6.0 * centre
                )
                value = 2.0 * centre - there[z] + cone_kappa[z] * spread
                if z == 0:
                    value = value + force_gain * cone_force[...]
                    for i in range(2):
                        motion[i, pl.ds(step, rows, stride=STEPS), :] = value[
                            STEPS : STEPS + rows, i * 128 : (i + 1) * 128
                        ]
                there[z] = value

    planes = depth // CHUNKS

    def halo(slot, part, side, arriving=False):
        place = side if arriving else side ^ 1
        if side < 2:
            layers = pl.ds(part * planes, planes)
            source = x_send.at[slot, side, :, layers]
            target = x_recv.at[slot, place, :, layers]
        else:
            source, target = y_send.at[slot, part], y_recv.at[slot, part, place - 2]
        return pltpu.make_async_remote_copy(
            src_ref=source,
            dst_ref=target,
            send_sem=halo_send.at[slot, part, side],
            recv_sem=halo_recv.at[slot, part, place],
            device_id=neighbour[side],
            device_id_type=MESH,
        )

    def send_halo(slot, part):
        for side in range(4):

            @pl.when(has[side])
            def _():
                halo(slot, part, side).start()

    def wait_halo(slot, part):
        for side in range(4):

            @pl.when(has[side])
            def _():
                halo(slot, part, side, True).wait_recv()

    lane = lax.broadcasted_iota(jnp.int32, (rows, 128), 1)
    first_lane, last_lane = lane == 0, lane == 127
    odd_lane = (lane % 2) == 1
    pair_of = lane // 2
    eight = lax.broadcasted_iota(jnp.int32, (8, 128), 0)
    no_edges = jnp.zeros((rows, 128), f32)

    def edge_rows(slot, z, i, value):
        x_send[slot, 0, i, pl.ds(z, 1), :] = value[0:1]
        x_send[slot, 1, i, pl.ds(z, 1), :] = value[rows - 1 : rows]

    def pack(edges, z, low, high):
        both = pltpu.roll(jnp.where(first_lane, low, high), 2 * z + 1, 1)
        return jnp.where(pair_of == z, both, edges)

    def plane(z, shift=0):
        return pl.ds(PAD + z * rows + shift, rows)

    def aligned(z):
        return pl.ds(pl.multiple_of(PAD + z * rows, 8), rows)

    def advance_planes(step, here, there, layers, edges, sides):
        results = []
        for z, top in layers:
            fresh = []
            halves = [here[0, aligned(z), :], here[1, aligned(z), :]]
            turned = [pltpu.roll(half, 1, 1) for half in halves]
            back = [pltpu.roll(half, 127, 1) for half in halves]
            beside = pltpu.roll(sides, 127 - 2 * z, 1)
            lows = [
                jnp.where(first_lane, beside, turned[0]),
                jnp.where(first_lane, turned[0], turned[1]),
            ]
            highs = [
                jnp.where(last_lane, back[1], back[0]),
                jnp.where(last_lane, beside, back[1]),
            ]
            for i in range(2):
                centre = halves[i]
                north = here[i, plane(z, -1), :]
                south = here[i, plane(z, 1), :]
                edge = jnp.where(eight == 0, x_recv[step, 0, i, pl.ds(z, 1), :], north[0:8])
                north = jnp.concatenate([edge, north[8:]], 0)
                edge = jnp.where(
                    eight == 7, x_recv[step, 1, i, pl.ds(z, 1), :], south[rows - 8 :]
                )
                south = jnp.concatenate([south[: rows - 8], edge], 0)
                above = centre if top else here[i, aligned(z - 1), :]
                below = here[i, aligned(z + 1), :]
                spread = (north + south) + (lows[i] + highs[i]) + (above + below) - 6.0 * centre
                value = (
                    2.0 * centre - there[i, aligned(z), :] + kappa[i, aligned(z), :] * spread
                )
                if top:
                    value = value + force_gain * force[:, i * 128 : (i + 1) * 128]
                fresh.append(value)
            results.append(fresh)
        for (z, top), fresh in zip(layers, results):
            for i in range(2):
                there[i, aligned(z), :] = fresh[i]
                if step < STEPS - 1:
                    edge_rows(step + 1, z, i, fresh[i])
            if step < STEPS - 1:
                edges = pack(edges, z, fresh[0], fresh[1])
        return edges

    states = (soil_a, soil_b)

    def advance(step, part):
        here, there = states[step % 2], states[(step + 1) % 2]
        wait_halo(step, part)
        first, last = part * planes, (part + 1) * planes
        sides = jnp.where(
            odd_lane,
            pltpu.roll(y_recv[step, part, 0], 1, 1),
            pltpu.roll(y_recv[step, part, 1], 127, 1),
        )
        edges = no_edges
        if part == 0:
            layers = [(z, z == 0) for z in range(GROUP)]
            edges = advance_planes(step, here, there, layers, edges, sides)
            first = GROUP

        def some(g, kept):
            z = first + g * GROUP
            layers = [(z + i, False) for i in range(GROUP)]
            return advance_planes(step, here, there, layers, kept, sides)

        edges = lax.fori_loop(0, (last - first) // GROUP, some, edges)
        if step < STEPS - 1:
            y_send[step + 1, part] = edges
            send_halo(step + 1, part)

    def soil_step(step):
        for part in range(CHUNKS):
            advance(step, part)

    pl.semaphore_wait(barrier, n_gx + n_gy - 2)
    for side in range(2):

        @pl.when(has[side])
        def _():
            for copy in cone_x(side):
                copy.start()

    for copy in loads[9:11]:
        copy.wait()
    for part in range(CHUNKS):

        def first_edges(g, kept):
            for i in range(8):
                z = part * planes + g * 8 + i
                low, high = soil_a[0, aligned(z), :], soil_a[1, aligned(z), :]
                edge_rows(0, z, 0, low)
                edge_rows(0, z, 1, high)
                kept = pack(kept, z, low, high)
            return kept

        y_send[0, part] = lax.fori_loop(0, planes // 8, first_edges, no_edges)
        send_halo(0, part)

    for copy in loads[0:4]:
        copy.wait()
    stiff[...] = stiff[...] * jnp.where(
        flag[...] == 0, 1.0, jnp.where(flag[...] == 1, 0.6, 0.15)
    ).astype(f32)
    payload[...] = jnp.zeros((tiles, WIDE), f32)
    before = (
        lax.broadcasted_iota(jnp.int32, (BLOCK, BLOCK), 0)
        < lax.broadcasted_iota(jnp.int32, (BLOCK, BLOCK), 1)
    ).astype(f32).astype(bf16)
    tile_number = lax.broadcasted_iota(jnp.int32, (tiles, BLOCK), 0)
    slot_number = lax.broadcasted_iota(jnp.int32, (SLOTS, BLOCK), 0)
    storey = lax.broadcasted_iota(jnp.int32, (8, BLOCK), 0)

    def list_block(j, used):
        cols = pl.ds(pl.multiple_of(j * BLOCK, BLOCK), BLOCK)
        chosen = (tile_number == tile_ref[:, cols]).astype(f32)
        mark = chosen.astype(bf16)
        marks[:, cols] = mark
        earlier = nn(mark, before) + used
        rank = jnp.sum(chosen * earlier, 0, keepdims=True).astype(jnp.int32)
        rank_ref[:, cols] = rank
        k = stiff[0:8, cols]
        of_disp = jnp.zeros((8, BLOCK), f32)
        of_vel = jnp.zeros((8, BLOCK), f32)
        coefs = jnp.zeros((8, BLOCK), f32)
        for step in reversed(range(STEPS)):
            of_vel = of_vel + of_disp
            pull = k * (jnp.where(storey == 0, 1.0, pltpu.roll(of_vel, 1, 0)) - of_vel)
            of_disp = of_disp + pull - jnp.where(storey == 7, 0.0, pltpu.roll(pull, 7, 0))
            coefs = jnp.where(storey == step, -pull[0:1], coefs)
        scale = 1.0 / STEPS
        constant = scale * jnp.sum(
            of_disp * disp[0:8, cols] + of_vel * vel[0:8, cols], 0, keepdims=True
        )
        coefs = scale * coefs
        row = (cell_ref[:, cols] // 256).astype(f32)
        col = (cell_ref[:, cols] % 256).astype(f32)
        here = slot_number == rank

        def spread_out(coef, single):
            parts = [jnp.where(rank == d, coef, 0.0) for d in range(SLOTS)]
            parts += [jnp.where(here, value, 0.0) for value in single]
            parts.append(jnp.zeros((SLOTS * (4 - len(single)), BLOCK), f32))
            return jnp.concatenate(parts, 0).astype(bf16)

        coef_high = coefs.astype(bf16).astype(f32)
        constant_high = constant.astype(bf16).astype(f32)
        payload[...] += nt(mark, spread_out(coef_high, (constant_high, row, col))) + nt(
            mark, spread_out(coefs - coef_high, (constant - constant_high,))
        )
        return used + jnp.sum(chosen, 1, keepdims=True)

    lax.fori_loop(0, count // BLOCK, list_block, jnp.zeros((tiles, 1), f32))

    def along_x(k):
        return lax.rem(gx + k, n_gx)

    def along_y(k):
        return lax.rem(gy + k, n_gy)

    def stage_x(source_of, target, send_sem, recv_sem):
        copies = []
        for k in range(1, n_gx):
            peer = along_x(k)
            copy = pltpu.make_async_remote_copy(
                src_ref=source_of(peer),
                dst_ref=target.at[gx],
                send_sem=send_sem.at[k],
                recv_sem=recv_sem.at[k],
                device_id=(peer, gy),
                device_id_type=MESH,
            )
            copy.start()
            copies.append(copy)
        return copies

    def stage_y(source_of, target, send_sem, recv_sem):
        copies = []
        for k in range(1, n_gy):
            peer = along_y(k)
            copy = pltpu.make_async_remote_copy(
                src_ref=source_of(peer),
                dst_ref=target.at[gy],
                send_sem=send_sem.at[k],
                recv_sem=recv_sem.at[k],
                device_id=(gx, peer),
                device_id_type=MESH,
            )
            copy.start()
            copies.append(copy)
        return copies

    def arrived_x(target, send_sem, recv_sem):
        for k in range(1, n_gx):
            place = target.at[lax.rem(gx + n_gx - k, n_gx)]
            pltpu.make_async_remote_copy(
                src_ref=place,
                dst_ref=place,
                send_sem=send_sem.at[k],
                recv_sem=recv_sem.at[k],
                device_id=(along_x(k), gy),
                device_id_type=MESH,
            ).wait_recv()

    def arrived_y(target, send_sem, recv_sem):
        for k in range(1, n_gy):
            place = target.at[lax.rem(gy + n_gy - k, n_gy)]
            pltpu.make_async_remote_copy(
                src_ref=place,
                dst_ref=place,
                send_sem=send_sem.at[k],
                recv_sem=recv_sem.at[k],
                device_id=(gx, along_y(k)),
                device_id_type=MESH,
            ).wait_recv()

    sends = []
    sends += stage_x(
        lambda peer: payload.at[pl.ds(pl.multiple_of(peer * n_gy, n_gy), n_gy)],
        recv_one,
        one_send,
        one_recv,
    )
    recv_one[gx] = payload[pl.ds(pl.multiple_of(gx * n_gy, n_gy), n_gy), :]

    for copy in loads[4:9]:
        copy.wait()
    for side in range(2):

        @pl.when(has[side])
        def _():
            for copy in cone_x(side, True):
                copy.wait_recv()

    cone_edges()
    for side in range(2):

        @pl.when(has[2 + side])
        def _():
            cone_y(side).start()

    for copy in loads[11:]:
        copy.wait()
    soil_step(0)
    for side in range(2):

        @pl.when(has[2 + side])
        def _():
            cone_y(side, True).wait_recv()

    cone_sides()
    cone_steps()

    arrived_x(recv_one, one_send, one_recv)
    for q in range(n_gy):
        for s in range(n_gx):
            mid_one[q, pl.ds(s, 1), :] = recv_one[s, pl.ds(q, 1), :]
    sends += stage_y(lambda peer: mid_one.at[peer], request, two_send, two_recv)
    request[gy] = mid_one[gy]

    soil_step(1)
    soil_step(2)

    arrived_y(request, two_send, two_recv)
    for q in range(WIDE // 128):
        request_t[pl.ds(q * 128, 128), :] = (
            request[:, :, pl.ds(q * 128, 128)].reshape(tiles, 128).T
        )
    table = jnp.concatenate(split(jnp.concatenate([motion[0], motion[1]], 1)), 1)
    line_number = lax.broadcasted_iota(jnp.int32, (rows, 128), 0).astype(f32)

    column_number = lax.broadcasted_iota(jnp.int32, (256, 128), 0).astype(f32)
    LINES = 4

    def pick(group, unused):
        chosen = []
        for i in range(LINES):
            wanted = request_t[pl.ds(COL + group * LINES + i, 1), :]
            chosen.append((column_number == wanted).astype(f32).astype(bf16))
        chosen = jnp.concatenate(chosen, 1)
        hot[:, pl.ds(pl.multiple_of(group * LINES * 128, 128), LINES * 128)] = chosen
        found = nn(table, jnp.concatenate([chosen, chosen], 0))
        totals = []
        for i in range(LINES):
            wanted = request_t[pl.ds(ROW + group * LINES + i, 1), :]
            sums = [jnp.zeros((STEPS, 128), f32) for unused_part in range(4)]
            for r in range(rows):
                sums[r % 4] += jnp.where(
                    wanted == float(r),
                    found[r * STEPS : (r + 1) * STEPS, i * 128 : (i + 1) * 128],
                    0.0,
                )
            totals.append((sums[0] + sums[1]) + (sums[2] + sums[3]))
        size = LINES * STEPS
        picked[pl.ds(pl.multiple_of(group * size, size), size), :] = jnp.concatenate(totals, 0)
        return unused

    lax.fori_loop(0, SLOTS // LINES, pick, 0)
    for q in range(2):
        reply[:, :, pl.ds(q * 128, 128)] = (
            picked[pl.ds(q * 128, 128), :].T.reshape(n_gy, n_gx, 128)
        )
    sends += stage_y(lambda peer: reply.at[peer], recv_two, three_send, three_recv)
    recv_two[gy] = reply[gy]

    stores = []
    soil_step(3)

    LANDED = 8

    def land(group, total):
        cols = pl.ds(pl.multiple_of(group * LANDED * 128, 128), LANDED * 128)
        parts = []
        for i in range(LANDED):
            d = group * LANDED + i
            lines = pl.ds(pl.multiple_of(d * STEPS, STEPS), STEPS)
            mean = request_t[pl.ds(BASE + d, 1), :] + jnp.sum(
                request_t[lines, :] * picked[lines, :], 0, keepdims=True
            )
            parts.append(jnp.where(line_number == request_t[pl.ds(ROW + d, 1), :], mean, 0.0))
        values = jnp.concatenate(parts, 1)
        return total + nt(jnp.concatenate(split(values), 0), hot[:, cols])

    landed = lax.fori_loop(0, SLOTS // LANDED, land, jnp.zeros((2 * rows, 256), f32))
    base[...] = landed[:rows] + landed[rows:]
    stores.append(pltpu.make_async_copy(base, base_out, out_sem.at[0]))
    stores[-1].start()

    soil_step(4)
    arrived_y(recv_two, three_send, three_recv)
    for s in range(n_gx):
        for q in range(n_gy):
            mid_two[s, pl.ds(q, 1), :] = recv_two[q, pl.ds(s, 1), :]
    sends += stage_x(lambda peer: mid_two.at[peer], answer, four_send, four_recv)
    answer[gx] = mid_two[gx]
    soil_step(5)
    soil_step(6)
    arrived_x(answer, four_send, four_recv)

    answer_t = jnp.concatenate(
        [answer[:, :, pl.ds(q * 128, 128)].reshape(tiles, 128).T for q in range(2)], 0
    )
    decoded = jnp.concatenate(split(answer_t), 1)
    level = lax.broadcasted_iota(jnp.int32, (32, BLOCK), 0)

    def window(j, unused):
        cols = pl.ds(pl.multiple_of(j * BLOCK, BLOCK), BLOCK)
        mark = marks[:, cols]
        found = nn(decoded, jnp.concatenate([mark, mark], 0))
        rank = rank_ref[:, cols]
        ground = jnp.zeros((STEPS, BLOCK), f32)
        for d in range(SLOTS):
            ground += jnp.where(rank == d, found[d * STEPS : (d + 1) * STEPS], 0.0)
        k, place, speed = stiff[:, cols], disp[:, cols], vel[:, cols]
        for step in range(STEPS):
            beneath = jnp.where(level == 0, ground[step : step + 1], pltpu.roll(place, 1, 0))
            shear = k * (place - beneath)
            upper = jnp.where(level == 31, 0.0, pltpu.roll(shear, 31, 0))
            speed = speed + upper - shear
            place = place + speed
        disp_new[:, cols] = place
        vel_new[:, cols] = speed
        return unused

    lax.fori_loop(0, count // BLOCK, window, 0)
    stores.append(pltpu.make_async_copy(disp_new, disp_out, out_sem.at[1]))
    stores.append(pltpu.make_async_copy(vel_new, vel_out, out_sem.at[2]))
    for copy in stores[1:]:
        copy.start()

    soil_step(7)
    for state, output in ((states[STEPS % 2], next_hbm), (states[(STEPS + 1) % 2], before_hbm)):
        for i in range(2):
            stores.append(
                pltpu.make_async_copy(
                    state.at[i, pl.ds(PAD, cells)],
                    output.at[:, pl.ds(i * 128, 128)],
                    out_sem.at[len(stores)],
                )
            )
            stores[-1].start()
    for side in range(2):

        @pl.when(has[side])
        def _():
            for copy in cone_x(side):
                copy.wait_send()

        @pl.when(has[2 + side])
        def _():
            cone_y(side).wait_send()

    for copy in sends:
        copy.wait_send()
    for slot in range(STEPS):
        for part in range(CHUNKS):
            for side in range(4):

                @pl.when(has[side])
                def _():
                    halo(slot, part, side).wait_send()

    for copy in stores:
        copy.wait()


def hand_over(*refs):
    sources, targets, held, sems = refs[:5], refs[5:10], refs[10:15], refs[15:]
    ways = []
    for source, target, room in zip(sources, targets, held):
        pieces = 2 if source.shape[0] > 256 else 1
        size = source.shape[0] // pieces
        for i in range(pieces):
            part = pl.ds(i * size, size)
            ways.append((source.at[part], room.at[part], target.at[part]))
    reads = [pltpu.make_async_copy(a, b, sems[0].at[i]) for i, (a, b, c) in enumerate(ways)]
    writes = [pltpu.make_async_copy(b, c, sems[1].at[i]) for i, (a, b, c) in enumerate(ways)]
    for copy in reads:
        copy.start()
    for read, write in zip(reads, writes):
        read.wait()
        write.start()
    for copy in writes:
        copy.wait()


def shards(
    soil_now,
    soil_old,
    kappa,
    force_prev,
    storey_disp,
    storey_vel,
    stiffness,
    branch_flag,
    footprint_tile,
    footprint_cell,
):
    n_gx, n_gy = lax.axis_size("gx"), lax.axis_size("gy")
    depth, rows, wide = soil_now.shape
    storeys, count = storey_disp.shape
    tiles = n_gx * n_gy
    flat = (depth * rows, wide)
    around = rows + 2 * STEPS
    hbm = pl.BlockSpec(memory_space=pltpu.HBM)
    dma = pltpu.SemaphoreType.DMA
    vm = pltpu.VMEM
    out = pl.pallas_call(
        functools.partial(kernel, n_gx, n_gy, depth, rows),
        out_shape=(
            jax.ShapeDtypeStruct(flat, f32),
            jax.ShapeDtypeStruct(flat, f32),
            jax.ShapeDtypeStruct((storeys, count), f32),
            jax.ShapeDtypeStruct((storeys, count), f32),
            jax.ShapeDtypeStruct((rows, wide), f32),
        ),
        in_specs=[pl.BlockSpec(memory_space=pltpu.VMEM)] * 2 + [hbm] * 11,
        out_specs=(hbm,) * 5,
        scratch_shapes=[
            vm((2, PAD + flat[0] + rows, 128), f32),
            vm((2, PAD + flat[0] + rows, 128), f32),
            vm((2, PAD + flat[0], 128), f32),
            vm((rows, wide), f32),
            vm((storeys, count), f32),
            vm((storeys, count), f32),
            vm((storeys, count), f32),
            vm((storeys, count), jnp.int32),
            vm((storeys, count), f32),
            vm((storeys, count), f32),
            vm((rows, wide), f32),
            vm((STEPS, 2, 2, depth, 128), f32),
            vm((STEPS, 2, 2, depth, 128), f32),
            vm((STEPS, CHUNKS, rows, 128), f32),
            vm((STEPS, CHUNKS, 2, rows, 128), f32),
            vm((STEPS + 1, around, 384), f32),
            vm((STEPS, around, 384), f32),
            vm((STEPS, around, 384), f32),
            vm((around, 384), f32),
            vm((2, 2, around, 128), f32),
            vm((2, 2, around, 128), f32),
            vm((tiles, count), bf16),
            vm((1, count), jnp.int32),
            vm((tiles, WIDE), f32),
            vm((n_gx, n_gy, WIDE), f32),
            vm((n_gy, n_gx, WIDE), f32),
            vm((n_gy, n_gx, WIDE), f32),
            vm((WIDE, tiles), f32),
            vm((wide, SLOTS * tiles), bf16),
            vm((2, rows * STEPS, 128), f32),
            vm((SLOTS * STEPS, tiles), f32),
            vm((n_gy, n_gx, SLOTS * STEPS), f32),
            vm((n_gy, n_gx, SLOTS * STEPS), f32),
            vm((n_gx, n_gy, SLOTS * STEPS), f32),
            vm((n_gx, n_gy, SLOTS * STEPS), f32),
            dma((15,)),
            dma((7,)),
            dma((STEPS, CHUNKS, 4)),
            dma((STEPS, CHUNKS, 4)),
            dma((4, 2)),
            dma((4, 2)),
            dma((2,)),
            dma((2,)),
            dma((n_gx,)),
            dma((n_gx,)),
            dma((n_gy,)),
            dma((n_gy,)),
            dma((n_gy,)),
            dma((n_gy,)),
            dma((n_gx,)),
            dma((n_gx,)),
        ],
        compiler_params=pltpu.CompilerParams(
            collective_id=0, has_side_effects=True, vmem_limit_bytes=62 * 1024 * 1024
        ),
        cost_estimate=pl.CostEstimate(
            flops=4_000_000_000, bytes_accessed=10_000_000, transcendentals=0
        ),
    )(
        footprint_tile.reshape(1, count),
        footprint_cell.reshape(1, count),
        soil_now.reshape(flat),
        soil_old.reshape(flat),
        kappa.reshape(flat),
        soil_now,
        soil_old,
        kappa,
        force_prev,
        storey_disp,
        storey_vel,
        stiffness,
        branch_flag,
    )
    out = pl.pallas_call(
        hand_over,
        out_shape=tuple(jax.ShapeDtypeStruct(a.shape, a.dtype) for a in out),
        in_specs=[hbm] * 5,
        out_specs=(hbm,) * 5,
        scratch_shapes=[vm(a.shape, a.dtype) for a in out] + [dma((7,)), dma((7,))],
        compiler_params=pltpu.CompilerParams(vmem_limit_bytes=62 * 1024 * 1024),
    )(*out)
    return (
        out[0].reshape(soil_now.shape),
        out[1].reshape(soil_now.shape),
        out[2],
        out[3],
        out[4],
    )


def solution(mesh):
    return jax.shard_map(
        shards,
        mesh=mesh,
        in_specs=(
            P(None, "gx", "gy"),
            P(None, "gx", "gy"),
            P(None, "gx", "gy"),
            P("gx", "gy"),
            P(None, ("gx", "gy")),
            P(None, ("gx", "gy")),
            P(None, ("gx", "gy")),
            P(None, ("gx", "gy")),
            P(("gx", "gy"), None),
            P(("gx", "gy")),
        ),
        out_specs=(
            P(None, "gx", "gy"),
            P(None, "gx", "gy"),
            P(None, ("gx", "gy")),
            P(None, ("gx", "gy")),
            P("gx", "gy"),
        ),
        check_vma=False,
    )
```

```python
import functools

import jax
import jax.numpy as jnp
from jax import lax
from jax.experimental import pallas as pl
from jax.experimental.pallas import tpu as pltpu
from jax.sharding import PartitionSpec as P

STEPS = 8
force_gain = 0.05
f32, bf16 = jnp.float32, jnp.bfloat16
GROUP = 8
PAD = 8
CHUNKS = 2
SLOTS = 32
COEF, BASE, ROW, COL, WIDE = 0, 256, 288, 320, 384
BLOCK = 512
RANKED = 256
MESH = pl.DeviceIdType.MESH


def split(x):
    high = x.astype(bf16)
    return high, (x - high.astype(f32)).astype(bf16)


def nt(a, b):
    return lax.dot_general(a, b, (((1,), (1,)), ((), ())), preferred_element_type=f32)


def nn(a, b):
    return jnp.dot(a, b, preferred_element_type=f32)


def kernel(
    n_gx,
    n_gy,
    depth,
    rows,
    tile_ref,
    cell_ref,
    now_hbm,
    old_hbm,
    kappa_hbm,
    now_deep,
    old_deep,
    kappa_deep,
    force_hbm,
    disp_hbm,
    vel_hbm,
    stiff_hbm,
    flag_hbm,
    next_hbm,
    before_hbm,
    disp_out,
    vel_out,
    base_out,
    soil_a,
    soil_b,
    kappa,
    force,
    disp,
    vel,
    stiff,
    flag,
    disp_new,
    vel_new,
    base,
    x_send,
    x_recv,
    y_send,
    y_recv,
    cone_now,
    cone_old,
    cone_kappa,
    cone_force,
    cone_send,
    cone_recv,
    marks,
    rank_ref,
    payload,
    recv_one,
    mid_one,
    request,
    request_t,
    hot,
    motion,
    picked,
    reply,
    recv_two,
    mid_two,
    answer,
    in_sem,
    out_sem,
    halo_send,
    halo_recv,
    cone_x_send,
    cone_x_recv,
    cone_y_send,
    cone_y_recv,
    one_send,
    one_recv,
    two_send,
    two_recv,
    three_send,
    three_recv,
    four_send,
    four_recv,
):
    gx, gy = lax.axis_index("gx"), lax.axis_index("gy")
    tiles = n_gx * n_gy
    count = tile_ref.shape[1]
    cells = depth * rows

    loads = []
    main = (pl.ds(STEPS, rows), pl.ds(0, 256))
    pairs = [
        (now_hbm.at[:, pl.ds(i * 128, 128)], soil_a.at[i, pl.ds(PAD, cells)]) for i in range(2)
    ]
    pairs += [
        (disp_hbm, disp),
        (vel_hbm, vel),
        (stiff_hbm, stiff),
        (flag_hbm, flag),
        (force_hbm, force),
        (now_deep.at[pl.ds(0, STEPS + 1)], cone_now.at[:, main[0], main[1]]),
        (old_deep.at[pl.ds(0, STEPS)], cone_old.at[:, main[0], main[1]]),
        (kappa_deep.at[pl.ds(0, STEPS)], cone_kappa.at[:, main[0], main[1]]),
        (force_hbm, cone_force.at[main[0], main[1]]),
    ]
    for source, target in ((old_hbm, soil_b), (kappa_hbm, kappa)):
        for i in range(2):
            pairs.append((source.at[:, pl.ds(i * 128, 128)], target.at[i, pl.ds(PAD, cells)]))
    for i, (source, target) in enumerate(pairs):
        copy = pltpu.make_async_copy(source, target, in_sem.at[i])
        copy.start()
        loads.append(copy)

    barrier = pltpu.get_barrier_semaphore()
    for k in range(1, n_gx):
        pl.semaphore_signal(
            barrier, inc=1, device_id=(lax.rem(gx + k, n_gx), gy), device_id_type=MESH
        )
    for k in range(1, n_gy):
        pl.semaphore_signal(
            barrier, inc=1, device_id=(gx, lax.rem(gy + k, n_gy)), device_id_type=MESH
        )

    for ref in (soil_a, soil_b):
        ref[:, pl.ds(PAD + cells, rows), :] = jnp.zeros((2, rows, 128), f32)
    has = (gx > 0, gx < n_gx - 1, gy > 0, gy < n_gy - 1)
    outside = (pl.ds(0, STEPS), pl.ds(STEPS + rows, STEPS))
    for side in range(4):

        @pl.when(jnp.logical_not(has[side]))
        def _():
            if side < 2:
                x_recv[:, side] = jnp.zeros((STEPS, 2, depth, 128), f32)
                for ref in (cone_now, cone_old, cone_kappa):
                    ref[:, outside[side], pl.ds(0, 256)] = jnp.zeros(
                        (ref.shape[0], STEPS, 256), f32
                    )
                cone_force[outside[side], pl.ds(0, 256)] = jnp.zeros((STEPS, 256), f32)
            else:
                y_recv[:, :, side - 2] = jnp.zeros((STEPS, CHUNKS, rows, 128), f32)
                cone_recv[side - 2] = jnp.zeros(cone_recv.shape[1:], f32)

    neighbour = ((gx - 1, gy), (gx + 1, gy), (gx, gy - 1), (gx, gy + 1))

    def cone_x(side, arriving=False):
        copies = []
        sources = (
            now_deep.at[pl.ds(0, STEPS + 1)],
            old_deep.at[pl.ds(0, STEPS)],
            kappa_deep.at[pl.ds(0, STEPS)],
        )
        edge = pl.ds(0, STEPS) if side == 0 else pl.ds(rows - STEPS, STEPS)
        place = side if arriving else side ^ 1
        for i, target in enumerate((cone_now, cone_old, cone_kappa, cone_force)):
            if i < 3:
                source = sources[i].at[:, edge, :]
                target = target.at[:, outside[place], pl.ds(0, 256)]
            else:
                source = force_hbm.at[edge, :]
                target = target.at[outside[place], pl.ds(0, 256)]
            copies.append(
                pltpu.make_async_remote_copy(
                    src_ref=source,
                    dst_ref=target,
                    send_sem=cone_x_send.at[i, side],
                    recv_sem=cone_x_recv.at[i, place],
                    device_id=neighbour[side],
                    device_id_type=MESH,
                )
            )
        return copies

    def cone_y(side, arriving=False):
        place = side if arriving else side ^ 1
        return pltpu.make_async_remote_copy(
            src_ref=cone_send.at[side],
            dst_ref=cone_recv.at[place],
            send_sem=cone_y_send.at[side],
            recv_sem=cone_y_recv.at[place],
            device_id=neighbour[2 + side],
            device_id_type=MESH,
        )

    around = rows + 2 * STEPS
    cone_lane = lax.broadcasted_iota(jnp.int32, (around, 128), 1)
    each = [(cone_now, z) for z in range(STEPS + 1)]
    each += [(ref, z) for ref in (cone_old, cone_kappa) for z in range(STEPS)]
    each += [(cone_force, None)]
    width = 128 // STEPS

    def cone_layer(ref, z, cols):
        return ref[:, cols] if z is None else ref[z, :, cols]

    def cone_edges():
        for group in range(2):
            west = jnp.zeros((around, 128), f32)
            east = jnp.zeros((around, 128), f32)
            for slot, (ref, z) in enumerate(each[group * width : (group + 1) * width]):
                here = (cone_lane // STEPS) == slot
                low = cone_layer(ref, z, pl.ds(0, 128))
                high = cone_layer(ref, z, pl.ds(128, 128))
                low = pltpu.roll(low, slot * STEPS, 1) if slot else low
                west = jnp.where(here, low, west)
                high = pltpu.roll(high, (slot + 1) * STEPS, 1) if slot < width - 1 else high
                east = jnp.where(here, high, east)
            cone_send[0, group] = west
            cone_send[1, group] = east

    def cone_sides():
        for group in range(2):
            west, east = cone_recv[0, group], cone_recv[1, group]
            for slot, (ref, z) in enumerate(each[group * width : (group + 1) * width]):
                low = pltpu.roll(west, 128 - (slot + 1) * STEPS, 1) if slot < width - 1 else west
                high = pltpu.roll(east, 128 - slot * STEPS, 1) if slot else east
                value = jnp.where(
                    cone_lane >= 128 - STEPS, low, jnp.where(cone_lane < STEPS, high, 0.0)
                )
                if z is None:
                    ref[:, pl.ds(256, 128)] = value
                else:
                    ref[z, :, pl.ds(256, 128)] = value

    def cone_steps():
        for step in range(STEPS):
            here, there = (cone_now, cone_old) if step % 2 == 0 else (cone_old, cone_now)
            for z in range(STEPS - step):
                centre = here[z]
                above = centre if z == 0 else here[z - 1]
                spread = (
                    (pltpu.roll(centre, 1, 0) + pltpu.roll(centre, around - 1, 0))
                    + (pltpu.roll(centre, 1, 1) + pltpu.roll(centre, 383, 1))
                    + (above + here[z + 1])
                    - 6.0 * centre
                )
                value = 2.0 * centre - there[z] + cone_kappa[z] * spread
                if z == 0:
                    value = value + force_gain * cone_force[...]
                    for i in range(2):
                        motion[i, pl.ds(step, rows, stride=STEPS), :] = value[
                            STEPS : STEPS + rows, i * 128 : (i + 1) * 128
                        ]
                there[z] = value

    planes = depth // CHUNKS

    def halo(slot, part, side, arriving=False):
        place = side if arriving else side ^ 1
        if side < 2:
            layers = pl.ds(part * planes, planes)
            source = x_send.at[slot, side, :, layers]
            target = x_recv.at[slot, place, :, layers]
        else:
            source, target = y_send.at[slot, part], y_recv.at[slot, part, place - 2]
        return pltpu.make_async_remote_copy(
            src_ref=source,
            dst_ref=target,
            send_sem=halo_send.at[slot, part, side],
            recv_sem=halo_recv.at[slot, part, place],
            device_id=neighbour[side],
            device_id_type=MESH,
        )

    def send_halo(slot, part):
        for side in range(4):

            @pl.when(has[side])
            def _():
                halo(slot, part, side).start()

    def wait_halo(slot, part):
        for side in range(4):

            @pl.when(has[side])
            def _():
                halo(slot, part, side, True).wait_recv()

    lane = lax.broadcasted_iota(jnp.int32, (rows, 128), 1)
    first_lane, last_lane = lane == 0, lane == 127
    odd_lane = (lane % 2) == 1
    pair_of = lane // 2
    eight = lax.broadcasted_iota(jnp.int32, (8, 128), 0)
    no_edges = jnp.zeros((rows, 128), f32)

    def edge_rows(slot, z, i, value):
        x_send[slot, 0, i, pl.ds(z, 1), :] = value[0:1]
        x_send[slot, 1, i, pl.ds(z, 1), :] = value[rows - 1 : rows]

    def pack(edges, z, low, high):
        both = pltpu.roll(jnp.where(first_lane, low, high), 2 * z + 1, 1)
        return jnp.where(pair_of == z, both, edges)

    def plane(z, shift=0):
        return pl.ds(PAD + z * rows + shift, rows)

    def aligned(z):
        return pl.ds(pl.multiple_of(PAD + z * rows, 8), rows)

    def advance_planes(step, here, there, layers, sides):
        results = []
        for z, top in layers:
            fresh = []
            halves = [here[0, aligned(z), :], here[1, aligned(z), :]]
            turned = [pltpu.roll(half, 1, 1) for half in halves]
            back = [pltpu.roll(half, 127, 1) for half in halves]
            beside = pltpu.roll(sides, 127 - 2 * z, 1)
            lows = [
                jnp.where(first_lane, beside, turned[0]),
                jnp.where(first_lane, turned[0], turned[1]),
            ]
            highs = [
                jnp.where(last_lane, back[1], back[0]),
                jnp.where(last_lane, beside, back[1]),
            ]
            for i in range(2):
                centre = halves[i]
                north = here[i, plane(z, -1), :]
                south = here[i, plane(z, 1), :]
                edge = jnp.where(eight == 0, x_recv[step, 0, i, pl.ds(z, 1), :], north[0:8])
                north = jnp.concatenate([edge, north[8:]], 0)
                edge = jnp.where(
                    eight == 7, x_recv[step, 1, i, pl.ds(z, 1), :], south[rows - 8 :]
                )
                south = jnp.concatenate([south[: rows - 8], edge], 0)
                above = centre if top else here[i, aligned(z - 1), :]
                below = here[i, aligned(z + 1), :]
                spread = (north + south) + (lows[i] + highs[i]) + (above + below) - 6.0 * centre
                value = (
                    2.0 * centre - there[i, aligned(z), :] + kappa[i, aligned(z), :] * spread
                )
                if top:
                    value = value + force_gain * force[:, i * 128 : (i + 1) * 128]
                fresh.append(value)
            results.append(fresh)
        for (z, top), fresh in zip(layers, results):
            for i in range(2):
                there[i, aligned(z), :] = fresh[i]
                if step < STEPS - 1:
                    edge_rows(step + 1, z, i, fresh[i])

    states = (soil_a, soil_b)

    def advance(step, part):
        here, there = states[step % 2], states[(step + 1) % 2]
        wait_halo(step, part)
        first, last = part * planes, (part + 1) * planes
        sides = jnp.where(
            odd_lane,
            pltpu.roll(y_recv[step, part, 0], 1, 1),
            pltpu.roll(y_recv[step, part, 1], 127, 1),
        )
        if part == 0:
            advance_planes(step, here, there, [(z, z == 0) for z in range(GROUP)], sides)
            first = GROUP

        def behind(z, kept):
            if step < STEPS - 1:
                values = [
                    (z - i, there[0, aligned(z - i), :], there[1, aligned(z - i), :])
                    for i in range(GROUP, 0, -1)
                ]
                for layer, low, high in values:
                    kept = pack(kept, layer, low, high)
            return kept

        def some(g, kept):
            z = first + g * GROUP
            kept = behind(z, kept)
            advance_planes(step, here, there, [(z + i, False) for i in range(GROUP)], sides)
            return kept

        edges = lax.fori_loop(0, (last - first) // GROUP, some, no_edges)
        if step < STEPS - 1:
            y_send[step + 1, part] = behind(last, edges)
            send_halo(step + 1, part)

    def soil_step(step):
        for part in range(CHUNKS):
            advance(step, part)

    for copy in loads[0:2]:
        copy.wait()
    for part in range(CHUNKS):

        def first_edges(g, kept):
            for i in range(8):
                z = part * planes + g * 8 + i
                low, high = soil_a[0, aligned(z), :], soil_a[1, aligned(z), :]
                edge_rows(0, z, 0, low)
                edge_rows(0, z, 1, high)
                kept = pack(kept, z, low, high)
            return kept

        y_send[0, part] = lax.fori_loop(0, planes // 8, first_edges, no_edges)
    pl.semaphore_wait(barrier, n_gx + n_gy - 2)
    for part in range(CHUNKS):
        send_halo(0, part)
    for side in range(2):

        @pl.when(has[side])
        def _():
            for copy in cone_x(side):
                copy.start()

    for copy in loads[2:6]:
        copy.wait()
    stiff[...] = stiff[...] * jnp.where(
        flag[...] == 0, 1.0, jnp.where(flag[...] == 1, 0.6, 0.15)
    ).astype(f32)
    payload[...] = jnp.zeros((tiles, WIDE), f32)
    before = (
        lax.broadcasted_iota(jnp.int32, (RANKED, RANKED), 0)
        < lax.broadcasted_iota(jnp.int32, (RANKED, RANKED), 1)
    ).astype(f32).astype(bf16)
    tile_number = lax.broadcasted_iota(jnp.int32, (tiles, BLOCK), 0)
    slot_number = lax.broadcasted_iota(jnp.int32, (SLOTS, BLOCK), 0)
    storey = lax.broadcasted_iota(jnp.int32, (8, BLOCK), 0)

    def list_block(j, used):
        cols = pl.ds(pl.multiple_of(j * BLOCK, BLOCK), BLOCK)
        chosen = (tile_number == tile_ref[:, cols]).astype(f32)
        mark = chosen.astype(bf16)
        marks[:, cols] = mark
        earlier = []
        for i in range(0, BLOCK, RANKED):
            earlier.append(nn(mark[:, i : i + RANKED], before) + used)
            used = used + jnp.sum(chosen[:, i : i + RANKED], 1, keepdims=True)
        earlier = jnp.concatenate(earlier, 1)
        rank = jnp.sum(chosen * earlier, 0, keepdims=True).astype(jnp.int32)
        rank_ref[:, cols] = rank
        k = stiff[0:8, cols]
        of_disp = jnp.zeros((8, BLOCK), f32)
        of_vel = jnp.zeros((8, BLOCK), f32)
        coefs = jnp.zeros((8, BLOCK), f32)
        for step in reversed(range(STEPS)):
            of_vel = of_vel + of_disp
            pull = k * (jnp.where(storey == 0, 1.0, pltpu.roll(of_vel, 1, 0)) - of_vel)
            of_disp = of_disp + pull - jnp.where(storey == 7, 0.0, pltpu.roll(pull, 7, 0))
            coefs = jnp.where(storey == step, -pull[0:1], coefs)
        scale = 1.0 / STEPS
        constant = scale * jnp.sum(
            of_disp * disp[0:8, cols] + of_vel * vel[0:8, cols], 0, keepdims=True
        )
        coefs = scale * coefs
        row = (cell_ref[:, cols] // 256).astype(f32)
        col = (cell_ref[:, cols] % 256).astype(f32)
        here = slot_number == rank

        def spread_out(coef, single):
            parts = [jnp.where(rank == d, coef, 0.0) for d in range(SLOTS)]
            parts += [jnp.where(here, value, 0.0) for value in single]
            parts.append(jnp.zeros((SLOTS * (4 - len(single)), BLOCK), f32))
            return jnp.concatenate(parts, 0).astype(bf16)

        coef_high = coefs.astype(bf16).astype(f32)
        constant_high = constant.astype(bf16).astype(f32)
        payload[...] += nt(mark, spread_out(coef_high, (constant_high, row, col))) + nt(
            mark, spread_out(coefs - coef_high, (constant - constant_high,))
        )
        return used

    blocks = count // BLOCK
    used = lax.fori_loop(0, blocks // 2, list_block, jnp.zeros((tiles, 1), f32))

    def along_x(k):
        return lax.rem(gx + k, n_gx)

    def along_y(k):
        return lax.rem(gy + k, n_gy)

    def stage_x(source_of, target, send_sem, recv_sem):
        copies = []
        for k in range(1, n_gx):
            peer = along_x(k)
            copy = pltpu.make_async_remote_copy(
                src_ref=source_of(peer),
                dst_ref=target.at[gx],
                send_sem=send_sem.at[k],
                recv_sem=recv_sem.at[k],
                device_id=(peer, gy),
                device_id_type=MESH,
            )
            copy.start()
            copies.append(copy)
        return copies

    def stage_y(source_of, target, send_sem, recv_sem):
        copies = []
        for k in range(1, n_gy):
            peer = along_y(k)
            copy = pltpu.make_async_remote_copy(
                src_ref=source_of(peer),
                dst_ref=target.at[gy],
                send_sem=send_sem.at[k],
                recv_sem=recv_sem.at[k],
                device_id=(gx, peer),
                device_id_type=MESH,
            )
            copy.start()
            copies.append(copy)
        return copies

    def arrived_x(target, send_sem, recv_sem):
        for k in range(1, n_gx):
            place = target.at[lax.rem(gx + n_gx - k, n_gx)]
            pltpu.make_async_remote_copy(
                src_ref=place,
                dst_ref=place,
                send_sem=send_sem.at[k],
                recv_sem=recv_sem.at[k],
                device_id=(along_x(k), gy),
                device_id_type=MESH,
            ).wait_recv()

    def arrived_y(target, send_sem, recv_sem):
        for k in range(1, n_gy):
            place = target.at[lax.rem(gy + n_gy - k, n_gy)]
            pltpu.make_async_remote_copy(
                src_ref=place,
                dst_ref=place,
                send_sem=send_sem.at[k],
                recv_sem=recv_sem.at[k],
                device_id=(gx, along_y(k)),
                device_id_type=MESH,
            ).wait_recv()

    for copy in loads[6:]:
        copy.wait()
    soil_step(0)
    lax.fori_loop(blocks // 2, blocks, list_block, used)
    sends = []
    sends += stage_x(
        lambda peer: payload.at[pl.ds(pl.multiple_of(peer * n_gy, n_gy), n_gy)],
        recv_one,
        one_send,
        one_recv,
    )
    recv_one[gx] = payload[pl.ds(pl.multiple_of(gx * n_gy, n_gy), n_gy), :]

    for side in range(2):

        @pl.when(has[side])
        def _():
            for copy in cone_x(side, True):
                copy.wait_recv()

    cone_edges()
    for side in range(2):

        @pl.when(has[2 + side])
        def _():
            cone_y(side).start()

    soil_step(1)

    arrived_x(recv_one, one_send, one_recv)
    for q in range(n_gy):
        for s in range(n_gx):
            mid_one[q, pl.ds(s, 1), :] = recv_one[s, pl.ds(q, 1), :]
    sends += stage_y(lambda peer: mid_one.at[peer], request, two_send, two_recv)
    request[gy] = mid_one[gy]

    soil_step(2)

    for side in range(2):

        @pl.when(has[2 + side])
        def _():
            cone_y(side, True).wait_recv()

    cone_sides()
    cone_steps()
    soil_step(3)

    arrived_y(request, two_send, two_recv)
    for q in range(WIDE // 128):
        request_t[pl.ds(q * 128, 128), :] = (
            request[:, :, pl.ds(q * 128, 128)].reshape(tiles, 128).T
        )
    table = jnp.concatenate(split(jnp.concatenate([motion[0], motion[1]], 1)), 1)
    line_number = lax.broadcasted_iota(jnp.int32, (rows, 128), 0).astype(f32)

    column_number = lax.broadcasted_iota(jnp.int32, (256, 128), 0).astype(f32)
    LINES = 4

    def pick(group, unused):
        chosen = []
        for i in range(LINES):
            wanted = request_t[pl.ds(COL + group * LINES + i, 1), :]
            chosen.append((column_number == wanted).astype(f32).astype(bf16))
        chosen = jnp.concatenate(chosen, 1)
        hot[:, pl.ds(pl.multiple_of(group * LINES * 128, 128), LINES * 128)] = chosen
        found = nn(table, jnp.concatenate([chosen, chosen], 0))
        totals = []
        for i in range(LINES):
            wanted = request_t[pl.ds(ROW + group * LINES + i, 1), :]
            sums = [jnp.zeros((STEPS, 128), f32) for unused_part in range(4)]
            for r in range(rows):
                sums[r % 4] += jnp.where(
                    wanted == float(r),
                    found[r * STEPS : (r + 1) * STEPS, i * 128 : (i + 1) * 128],
                    0.0,
                )
            totals.append((sums[0] + sums[1]) + (sums[2] + sums[3]))
        size = LINES * STEPS
        picked[pl.ds(pl.multiple_of(group * size, size), size), :] = jnp.concatenate(totals, 0)
        return unused

    lax.fori_loop(0, SLOTS // LINES, pick, 0)
    for q in range(2):
        reply[:, :, pl.ds(q * 128, 128)] = (
            picked[pl.ds(q * 128, 128), :].T.reshape(n_gy, n_gx, 128)
        )
    sends += stage_y(lambda peer: reply.at[peer], recv_two, three_send, three_recv)
    recv_two[gy] = reply[gy]

    stores = []
    soil_step(4)

    LANDED = 8

    def land(group, total):
        cols = pl.ds(pl.multiple_of(group * LANDED * 128, 128), LANDED * 128)
        parts = []
        for i in range(LANDED):
            d = group * LANDED + i
            lines = pl.ds(pl.multiple_of(d * STEPS, STEPS), STEPS)
            mean = request_t[pl.ds(BASE + d, 1), :] + jnp.sum(
                request_t[lines, :] * picked[lines, :], 0, keepdims=True
            )
            parts.append(jnp.where(line_number == request_t[pl.ds(ROW + d, 1), :], mean, 0.0))
        values = jnp.concatenate(parts, 1)
        return total + nt(jnp.concatenate(split(values), 0), hot[:, cols])

    landed = lax.fori_loop(0, SLOTS // LANDED, land, jnp.zeros((2 * rows, 256), f32))
    base[...] = landed[:rows] + landed[rows:]
    stores.append(pltpu.make_async_copy(base, base_out, out_sem.at[0]))
    stores[-1].start()

    soil_step(5)
    arrived_y(recv_two, three_send, three_recv)
    for s in range(n_gx):
        for q in range(n_gy):
            mid_two[s, pl.ds(q, 1), :] = recv_two[q, pl.ds(s, 1), :]
    sends += stage_x(lambda peer: mid_two.at[peer], answer, four_send, four_recv)
    answer[gx] = mid_two[gx]
    soil_step(6)
    arrived_x(answer, four_send, four_recv)

    answer_t = jnp.concatenate(
        [answer[:, :, pl.ds(q * 128, 128)].reshape(tiles, 128).T for q in range(2)], 0
    )
    decoded = jnp.concatenate(split(answer_t), 1)
    level = lax.broadcasted_iota(jnp.int32, (32, BLOCK), 0)

    def window(j, unused):
        cols = pl.ds(pl.multiple_of(j * BLOCK, BLOCK), BLOCK)
        mark = marks[:, cols]
        found = nn(decoded, jnp.concatenate([mark, mark], 0))
        rank = rank_ref[:, cols]
        ground = jnp.zeros((STEPS, BLOCK), f32)
        for d in range(SLOTS):
            ground += jnp.where(rank == d, found[d * STEPS : (d + 1) * STEPS], 0.0)
        k, place, speed = stiff[:, cols], disp[:, cols], vel[:, cols]
        for step in range(STEPS):
            beneath = jnp.where(level == 0, ground[step : step + 1], pltpu.roll(place, 1, 0))
            shear = k * (place - beneath)
            upper = jnp.where(level == 31, 0.0, pltpu.roll(shear, 31, 0))
            speed = speed + upper - shear
            place = place + speed
        disp_new[:, cols] = place
        vel_new[:, cols] = speed
        return unused

    lax.fori_loop(0, count // BLOCK, window, 0)
    stores.append(pltpu.make_async_copy(disp_new, disp_out, out_sem.at[1]))
    stores.append(pltpu.make_async_copy(vel_new, vel_out, out_sem.at[2]))
    for copy in stores[1:]:
        copy.start()

    soil_step(7)
    for state, output in ((states[STEPS % 2], next_hbm), (states[(STEPS + 1) % 2], before_hbm)):
        for i in range(2):
            stores.append(
                pltpu.make_async_copy(
                    state.at[i, pl.ds(PAD, cells)],
                    output.at[:, pl.ds(i * 128, 128)],
                    out_sem.at[len(stores)],
                )
            )
            stores[-1].start()
    for side in range(2):

        @pl.when(has[side])
        def _():
            for copy in cone_x(side):
                copy.wait_send()

        @pl.when(has[2 + side])
        def _():
            cone_y(side).wait_send()

    for copy in sends:
        copy.wait_send()
    for slot in range(STEPS):
        for part in range(CHUNKS):
            for side in range(4):

                @pl.when(has[side])
                def _():
                    halo(slot, part, side).wait_send()

    for copy in stores:
        copy.wait()


def hand_over(*refs):
    sources, targets, held, sems = refs[:5], refs[5:10], refs[10:15], refs[15:]
    ways = []
    for source, target, room in zip(sources, targets, held):
        pieces = 2 if source.shape[0] > 256 else 1
        size = source.shape[0] // pieces
        for i in range(pieces):
            part = pl.ds(i * size, size)
            ways.append((source.at[part], room.at[part], target.at[part]))
    reads = [pltpu.make_async_copy(a, b, sems[0].at[i]) for i, (a, b, c) in enumerate(ways)]
    writes = [pltpu.make_async_copy(b, c, sems[1].at[i]) for i, (a, b, c) in enumerate(ways)]
    for copy in reads:
        copy.start()
    for read, write in zip(reads, writes):
        read.wait()
        write.start()
    for copy in writes:
        copy.wait()


def shards(
    soil_now,
    soil_old,
    kappa,
    force_prev,
    storey_disp,
    storey_vel,
    stiffness,
    branch_flag,
    footprint_tile,
    footprint_cell,
):
    n_gx, n_gy = lax.axis_size("gx"), lax.axis_size("gy")
    depth, rows, wide = soil_now.shape
    storeys, count = storey_disp.shape
    tiles = n_gx * n_gy
    flat = (depth * rows, wide)
    around = rows + 2 * STEPS
    hbm = pl.BlockSpec(memory_space=pltpu.HBM)
    dma = pltpu.SemaphoreType.DMA
    vm = pltpu.VMEM
    out = pl.pallas_call(
        functools.partial(kernel, n_gx, n_gy, depth, rows),
        out_shape=(
            jax.ShapeDtypeStruct(flat, f32),
            jax.ShapeDtypeStruct(flat, f32),
            jax.ShapeDtypeStruct((storeys, count), f32),
            jax.ShapeDtypeStruct((storeys, count), f32),
            jax.ShapeDtypeStruct((rows, wide), f32),
        ),
        in_specs=[pl.BlockSpec(memory_space=pltpu.VMEM)] * 2 + [hbm] * 11,
        out_specs=(hbm,) * 5,
        scratch_shapes=[
            vm((2, PAD + flat[0] + rows, 128), f32),
            vm((2, PAD + flat[0] + rows, 128), f32),
            vm((2, PAD + flat[0], 128), f32),
            vm((rows, wide), f32),
            vm((storeys, count), f32),
            vm((storeys, count), f32),
            vm((storeys, count), f32),
            vm((storeys, count), jnp.int32),
            vm((storeys, count), f32),
            vm((storeys, count), f32),
            vm((rows, wide), f32),
            vm((STEPS, 2, 2, depth, 128), f32),
            vm((STEPS, 2, 2, depth, 128), f32),
            vm((STEPS, CHUNKS, rows, 128), f32),
            vm((STEPS, CHUNKS, 2, rows, 128), f32),
            vm((STEPS + 1, around, 384), f32),
            vm((STEPS, around, 384), f32),
            vm((STEPS, around, 384), f32),
            vm((around, 384), f32),
            vm((2, 2, around, 128), f32),
            vm((2, 2, around, 128), f32),
            vm((tiles, count), bf16),
            vm((1, count), jnp.int32),
            vm((tiles, WIDE), f32),
            vm((n_gx, n_gy, WIDE), f32),
            vm((n_gy, n_gx, WIDE), f32),
            vm((n_gy, n_gx, WIDE), f32),
            vm((WIDE, tiles), f32),
            vm((wide, SLOTS * tiles), bf16),
            vm((2, rows * STEPS, 128), f32),
            vm((SLOTS * STEPS, tiles), f32),
            vm((n_gy, n_gx, SLOTS * STEPS), f32),
            vm((n_gy, n_gx, SLOTS * STEPS), f32),
            vm((n_gx, n_gy, SLOTS * STEPS), f32),
            vm((n_gx, n_gy, SLOTS * STEPS), f32),
            dma((15,)),
            dma((7,)),
            dma((STEPS, CHUNKS, 4)),
            dma((STEPS, CHUNKS, 4)),
            dma((4, 2)),
            dma((4, 2)),
            dma((2,)),
            dma((2,)),
            dma((n_gx,)),
            dma((n_gx,)),
            dma((n_gy,)),
            dma((n_gy,)),
            dma((n_gy,)),
            dma((n_gy,)),
            dma((n_gx,)),
            dma((n_gx,)),
        ],
        compiler_params=pltpu.CompilerParams(
            collective_id=0, has_side_effects=True, vmem_limit_bytes=62 * 1024 * 1024
        ),
        cost_estimate=pl.CostEstimate(
            flops=4_000_000_000, bytes_accessed=10_000_000, transcendentals=0
        ),
    )(
        footprint_tile.reshape(1, count),
        footprint_cell.reshape(1, count),
        soil_now.reshape(flat),
        soil_old.reshape(flat),
        kappa.reshape(flat),
        soil_now,
        soil_old,
        kappa,
        force_prev,
        storey_disp,
        storey_vel,
        stiffness,
        branch_flag,
    )
    out = pl.pallas_call(
        hand_over,
        out_shape=tuple(jax.ShapeDtypeStruct(a.shape, a.dtype) for a in out),
        in_specs=[hbm] * 5,
        out_specs=(hbm,) * 5,
        scratch_shapes=[vm(a.shape, a.dtype) for a in out] + [dma((7,)), dma((7,))],
        compiler_params=pltpu.CompilerParams(vmem_limit_bytes=62 * 1024 * 1024),
    )(*out)
    return (
        out[0].reshape(soil_now.shape),
        out[1].reshape(soil_now.shape),
        out[2],
        out[3],
        out[4],
    )


def solution(mesh):
    return jax.shard_map(
        shards,
        mesh=mesh,
        in_specs=(
            P(None, "gx", "gy"),
            P(None, "gx", "gy"),
            P(None, "gx", "gy"),
            P("gx", "gy"),
            P(None, ("gx", "gy")),
            P(None, ("gx", "gy")),
            P(None, ("gx", "gy")),
            P(None, ("gx", "gy")),
            P(("gx", "gy"), None),
            P(("gx", "gy")),
        ),
        out_specs=(
            P(None, "gx", "gy"),
            P(None, "gx", "gy"),
            P(None, ("gx", "gy")),
            P(None, ("gx", "gy")),
            P("gx", "gy"),
        ),
        check_vma=False,
    )
```

```python
import functools

import jax
import jax.numpy as jnp
from jax import lax
from jax.experimental import pallas as pl
from jax.experimental.pallas import tpu as pltpu
from jax.sharding import PartitionSpec as P

STEPS = 8
force_gain = 0.05
f32, bf16 = jnp.float32, jnp.bfloat16
GROUP = 8
PAD = 8
CHUNKS = 2
SLOTS = 32
COEF, BASE, ROW, COL, WIDE = 0, 256, 288, 320, 384
BLOCK = 512
RANKED = 256
MESH = pl.DeviceIdType.MESH


def split(x):
    high = x.astype(bf16)
    return high, (x - high.astype(f32)).astype(bf16)


def nt(a, b):
    return lax.dot_general(a, b, (((1,), (1,)), ((), ())), preferred_element_type=f32)


def nn(a, b):
    return jnp.dot(a, b, preferred_element_type=f32)


def kernel(
    n_gx,
    n_gy,
    depth,
    rows,
    tile_ref,
    cell_ref,
    now_hbm,
    old_hbm,
    kappa_hbm,
    now_deep,
    old_deep,
    kappa_deep,
    force_hbm,
    disp_hbm,
    vel_hbm,
    stiff_hbm,
    flag_hbm,
    next_hbm,
    before_hbm,
    disp_out,
    vel_out,
    base_out,
    soil_a,
    soil_b,
    kappa,
    force,
    disp,
    vel,
    stiff,
    flag,
    disp_new,
    vel_new,
    base,
    x_send,
    x_recv,
    y_send,
    y_recv,
    cone_now,
    cone_old,
    cone_kappa,
    cone_force,
    cone_send,
    cone_recv,
    marks,
    rank_ref,
    payload,
    recv_one,
    mid_one,
    request,
    request_t,
    hot,
    motion,
    picked,
    reply,
    recv_two,
    mid_two,
    answer,
    in_sem,
    out_sem,
    halo_send,
    halo_recv,
    cone_x_send,
    cone_x_recv,
    cone_y_send,
    cone_y_recv,
    one_send,
    one_recv,
    two_send,
    two_recv,
    three_send,
    three_recv,
    four_send,
    four_recv,
):
    gx, gy = lax.axis_index("gx"), lax.axis_index("gy")
    tiles = n_gx * n_gy
    count = tile_ref.shape[1]
    cells = depth * rows

    loads = []
    main = (pl.ds(STEPS, rows), pl.ds(0, 256))
    pairs = [
        (now_hbm.at[:, pl.ds(i * 128, 128)], soil_a.at[i, pl.ds(PAD, cells)]) for i in range(2)
    ]
    pairs += [
        (disp_hbm, disp),
        (vel_hbm, vel),
        (stiff_hbm, stiff),
        (flag_hbm, flag),
        (force_hbm, force),
        (now_deep.at[pl.ds(0, STEPS + 1)], cone_now.at[:, main[0], main[1]]),
        (old_deep.at[pl.ds(0, STEPS)], cone_old.at[:, main[0], main[1]]),
        (kappa_deep.at[pl.ds(0, STEPS)], cone_kappa.at[:, main[0], main[1]]),
        (force_hbm, cone_force.at[main[0], main[1]]),
    ]
    for source, target in ((old_hbm, soil_b), (kappa_hbm, kappa)):
        for i in range(2):
            pairs.append((source.at[:, pl.ds(i * 128, 128)], target.at[i, pl.ds(PAD, cells)]))
    for i, (source, target) in enumerate(pairs):
        copy = pltpu.make_async_copy(source, target, in_sem.at[i])
        copy.start()
        loads.append(copy)

    barrier = pltpu.get_barrier_semaphore()
    for k in range(1, n_gx):
        pl.semaphore_signal(
            barrier, inc=1, device_id=(lax.rem(gx + k, n_gx), gy), device_id_type=MESH
        )
    for k in range(1, n_gy):
        pl.semaphore_signal(
            barrier, inc=1, device_id=(gx, lax.rem(gy + k, n_gy)), device_id_type=MESH
        )

    for ref in (soil_a, soil_b):
        ref[:, pl.ds(PAD + cells, rows), :] = jnp.zeros((2, rows, 128), f32)
    has = (gx > 0, gx < n_gx - 1, gy > 0, gy < n_gy - 1)
    outside = (pl.ds(0, STEPS), pl.ds(STEPS + rows, STEPS))
    for side in range(4):

        @pl.when(jnp.logical_not(has[side]))
        def _():
            if side < 2:
                x_recv[:, side] = jnp.zeros((STEPS, 2, depth, 128), f32)
                for ref in (cone_now, cone_old, cone_kappa):
                    ref[:, outside[side], pl.ds(0, 256)] = jnp.zeros(
                        (ref.shape[0], STEPS, 256), f32
                    )
                cone_force[outside[side], pl.ds(0, 256)] = jnp.zeros((STEPS, 256), f32)
            else:
                y_recv[:, :, side - 2] = jnp.zeros((STEPS, CHUNKS, rows, 128), f32)
                cone_recv[side - 2] = jnp.zeros(cone_recv.shape[1:], f32)

    neighbour = ((gx - 1, gy), (gx + 1, gy), (gx, gy - 1), (gx, gy + 1))

    def cone_x(side, arriving=False):
        copies = []
        sources = (
            now_deep.at[pl.ds(0, STEPS + 1)],
            old_deep.at[pl.ds(0, STEPS)],
            kappa_deep.at[pl.ds(0, STEPS)],
        )
        edge = pl.ds(0, STEPS) if side == 0 else pl.ds(rows - STEPS, STEPS)
        place = side if arriving else side ^ 1
        for i, target in enumerate((cone_now, cone_old, cone_kappa, cone_force)):
            if i < 3:
                source = sources[i].at[:, edge, :]
                target = target.at[:, outside[place], pl.ds(0, 256)]
            else:
                source = force_hbm.at[edge, :]
                target = target.at[outside[place], pl.ds(0, 256)]
            copies.append(
                pltpu.make_async_remote_copy(
                    src_ref=source,
                    dst_ref=target,
                    send_sem=cone_x_send.at[i, side],
                    recv_sem=cone_x_recv.at[i, place],
                    device_id=neighbour[side],
                    device_id_type=MESH,
                )
            )
        return copies

    def cone_y(side, arriving=False):
        place = side if arriving else side ^ 1
        return pltpu.make_async_remote_copy(
            src_ref=cone_send.at[side],
            dst_ref=cone_recv.at[place],
            send_sem=cone_y_send.at[side],
            recv_sem=cone_y_recv.at[place],
            device_id=neighbour[2 + side],
            device_id_type=MESH,
        )

    around = rows + 2 * STEPS
    cone_lane = lax.broadcasted_iota(jnp.int32, (around, 128), 1)
    each = [(cone_now, z) for z in range(STEPS + 1)]
    each += [(ref, z) for ref in (cone_old, cone_kappa) for z in range(STEPS)]
    each += [(cone_force, None)]
    width = 128 // STEPS

    def cone_layer(ref, z, cols):
        return ref[:, cols] if z is None else ref[z, :, cols]

    def cone_edges():
        for group in range(2):
            west = jnp.zeros((around, 128), f32)
            east = jnp.zeros((around, 128), f32)
            for slot, (ref, z) in enumerate(each[group * width : (group + 1) * width]):
                here = (cone_lane // STEPS) == slot
                low = cone_layer(ref, z, pl.ds(0, 128))
                high = cone_layer(ref, z, pl.ds(128, 128))
                low = pltpu.roll(low, slot * STEPS, 1) if slot else low
                west = jnp.where(here, low, west)
                high = pltpu.roll(high, (slot + 1) * STEPS, 1) if slot < width - 1 else high
                east = jnp.where(here, high, east)
            cone_send[0, group] = west
            cone_send[1, group] = east

    def cone_sides():
        for group in range(2):
            west, east = cone_recv[0, group], cone_recv[1, group]
            for slot, (ref, z) in enumerate(each[group * width : (group + 1) * width]):
                low = pltpu.roll(west, 128 - (slot + 1) * STEPS, 1) if slot < width - 1 else west
                high = pltpu.roll(east, 128 - slot * STEPS, 1) if slot else east
                value = jnp.where(
                    cone_lane >= 128 - STEPS, low, jnp.where(cone_lane < STEPS, high, 0.0)
                )
                if z is None:
                    ref[:, pl.ds(256, 128)] = value
                else:
                    ref[z, :, pl.ds(256, 128)] = value

    def cone_steps():
        for step in range(STEPS):
            here, there = (cone_now, cone_old) if step % 2 == 0 else (cone_old, cone_now)
            for z in range(STEPS - step):
                centre = here[z]
                above = centre if z == 0 else here[z - 1]
                spread = (
                    (pltpu.roll(centre, 1, 0) + pltpu.roll(centre, around - 1, 0))
                    + (pltpu.roll(centre, 1, 1) + pltpu.roll(centre, 383, 1))
                    + (above + here[z + 1])
                    - 6.0 * centre
                )
                value = 2.0 * centre - there[z] + cone_kappa[z] * spread
                if z == 0:
                    value = value + force_gain * cone_force[...]
                    for i in range(2):
                        motion[i, pl.ds(step, rows, stride=STEPS), :] = value[
                            STEPS : STEPS + rows, i * 128 : (i + 1) * 128
                        ]
                there[z] = value

    planes = depth // CHUNKS

    def halo(slot, part, side, arriving=False):
        place = side if arriving else side ^ 1
        if side < 2:
            layers = pl.ds(part * planes, planes)
            source = x_send.at[slot, side, :, layers]
            target = x_recv.at[slot, place, :, layers]
        else:
            source, target = y_send.at[slot, part], y_recv.at[slot, part, place - 2]
        return pltpu.make_async_remote_copy(
            src_ref=source,
            dst_ref=target,
            send_sem=halo_send.at[slot, part, side],
            recv_sem=halo_recv.at[slot, part, place],
            device_id=neighbour[side],
            device_id_type=MESH,
        )

    def send_halo(slot, part):
        for side in range(4):

            @pl.when(has[side])
            def _():
                halo(slot, part, side).start()

    def wait_halo(slot, part):
        for side in range(4):

            @pl.when(has[side])
            def _():
                halo(slot, part, side, True).wait_recv()

    lane = lax.broadcasted_iota(jnp.int32, (rows, 128), 1)
    first_lane, last_lane = lane == 0, lane == 127
    odd_lane = (lane % 2) == 1
    pair_of = lane // 2
    eight = lax.broadcasted_iota(jnp.int32, (8, 128), 0)
    no_edges = jnp.zeros((rows, 128), f32)

    def edge_rows(slot, z, i, value):
        x_send[slot, 0, i, pl.ds(z, 1), :] = value[0:1]
        x_send[slot, 1, i, pl.ds(z, 1), :] = value[rows - 1 : rows]

    def pack(edges, z, low, high):
        both = pltpu.roll(jnp.where(first_lane, low, high), 2 * z + 1, 1)
        return jnp.where(pair_of == z, both, edges)

    def plane(z, shift=0):
        return pl.ds(PAD + z * rows + shift, rows)

    def aligned(z):
        return pl.ds(pl.multiple_of(PAD + z * rows, 8), rows)

    def advance_planes(step, here, there, layers, sides):
        results = []
        for z, top in layers:
            fresh = []
            halves = [here[0, aligned(z), :], here[1, aligned(z), :]]
            turned = [pltpu.roll(half, 1, 1) for half in halves]
            back = [pltpu.roll(half, 127, 1) for half in halves]
            beside = pltpu.roll(sides, 127 - 2 * z, 1)
            lows = [
                jnp.where(first_lane, beside, turned[0]),
                jnp.where(first_lane, turned[0], turned[1]),
            ]
            highs = [
                jnp.where(last_lane, back[1], back[0]),
                jnp.where(last_lane, beside, back[1]),
            ]
            for i in range(2):
                centre = halves[i]
                north = here[i, plane(z, -1), :]
                south = here[i, plane(z, 1), :]
                edge = jnp.where(eight == 0, x_recv[step, 0, i, pl.ds(z, 1), :], north[0:8])
                north = jnp.concatenate([edge, north[8:]], 0)
                edge = jnp.where(
                    eight == 7, x_recv[step, 1, i, pl.ds(z, 1), :], south[rows - 8 :]
                )
                south = jnp.concatenate([south[: rows - 8], edge], 0)
                above = centre if top else here[i, aligned(z - 1), :]
                below = here[i, aligned(z + 1), :]
                spread = (north + south) + (lows[i] + highs[i]) + (above + below) - 6.0 * centre
                value = (
                    2.0 * centre - there[i, aligned(z), :] + kappa[i, aligned(z), :] * spread
                )
                if top:
                    value = value + force_gain * force[:, i * 128 : (i + 1) * 128]
                fresh.append(value)
            results.append(fresh)
        for (z, top), fresh in zip(layers, results):
            for i in range(2):
                there[i, aligned(z), :] = fresh[i]
                if step < STEPS - 1:
                    edge_rows(step + 1, z, i, fresh[i])

    states = (soil_a, soil_b)

    def advance(step, part):
        here, there = states[step % 2], states[(step + 1) % 2]
        wait_halo(step, part)
        first, last = part * planes, (part + 1) * planes
        sides = jnp.where(
            odd_lane,
            pltpu.roll(y_recv[step, part, 0], 1, 1),
            pltpu.roll(y_recv[step, part, 1], 127, 1),
        )
        if part == 0:
            advance_planes(step, here, there, [(z, z == 0) for z in range(GROUP)], sides)
            first = GROUP

        def behind(z, kept):
            if step < STEPS - 1:
                values = [
                    (z - i, there[0, aligned(z - i), :], there[1, aligned(z - i), :])
                    for i in range(GROUP, 0, -1)
                ]
                for layer, low, high in values:
                    kept = pack(kept, layer, low, high)
            return kept

        def some(g, kept):
            z = first + g * GROUP
            kept = behind(z, kept)
            advance_planes(step, here, there, [(z + i, False) for i in range(GROUP)], sides)
            return kept

        edges = lax.fori_loop(0, (last - first) // GROUP, some, no_edges)
        if step < STEPS - 1:
            y_send[step + 1, part] = behind(last, edges)
            send_halo(step + 1, part)

    def soil_step(step):
        for part in range(CHUNKS):
            advance(step, part)

    for copy in loads[0:2]:
        copy.wait()
    for part in range(CHUNKS):

        def first_edges(g, kept):
            for i in range(8):
                z = part * planes + g * 8 + i
                low, high = soil_a[0, aligned(z), :], soil_a[1, aligned(z), :]
                edge_rows(0, z, 0, low)
                edge_rows(0, z, 1, high)
                kept = pack(kept, z, low, high)
            return kept

        y_send[0, part] = lax.fori_loop(0, planes // 8, first_edges, no_edges)
    pl.semaphore_wait(barrier, n_gx + n_gy - 2)
    for part in range(CHUNKS):
        send_halo(0, part)
    for side in range(2):

        @pl.when(has[side])
        def _():
            for copy in cone_x(side):
                copy.start()

    for copy in loads[2:6]:
        copy.wait()
    stiff[...] = stiff[...] * jnp.where(
        flag[...] == 0, 1.0, jnp.where(flag[...] == 1, 0.6, 0.15)
    ).astype(f32)
    payload[...] = jnp.zeros((tiles, WIDE), f32)
    before = (
        lax.broadcasted_iota(jnp.int32, (RANKED, RANKED), 0)
        < lax.broadcasted_iota(jnp.int32, (RANKED, RANKED), 1)
    ).astype(f32).astype(bf16)
    tile_number = lax.broadcasted_iota(jnp.int32, (tiles, BLOCK), 0)
    slot_number = lax.broadcasted_iota(jnp.int32, (SLOTS, BLOCK), 0)
    storey = lax.broadcasted_iota(jnp.int32, (8, BLOCK), 0)

    def list_block(j, used):
        cols = pl.ds(pl.multiple_of(j * BLOCK, BLOCK), BLOCK)
        chosen = (tile_number == tile_ref[:, cols]).astype(f32)
        mark = chosen.astype(bf16)
        marks[:, cols] = mark
        earlier = []
        for i in range(0, BLOCK, RANKED):
            earlier.append(nn(mark[:, i : i + RANKED], before) + used)
            used = used + jnp.sum(chosen[:, i : i + RANKED], 1, keepdims=True)
        earlier = jnp.concatenate(earlier, 1)
        rank = jnp.sum(chosen * earlier, 0, keepdims=True).astype(jnp.int32)
        rank_ref[:, cols] = rank
        k = stiff[0:8, cols]
        of_disp = jnp.zeros((8, BLOCK), f32)
        of_vel = jnp.zeros((8, BLOCK), f32)
        coefs = jnp.zeros((8, BLOCK), f32)
        for step in reversed(range(STEPS)):
            of_vel = of_vel + of_disp
            pull = k * (jnp.where(storey == 0, 1.0, pltpu.roll(of_vel, 1, 0)) - of_vel)
            of_disp = of_disp + pull - jnp.where(storey == 7, 0.0, pltpu.roll(pull, 7, 0))
            coefs = jnp.where(storey == step, -pull[0:1], coefs)
        scale = 1.0 / STEPS
        constant = scale * jnp.sum(
            of_disp * disp[0:8, cols] + of_vel * vel[0:8, cols], 0, keepdims=True
        )
        coefs = scale * coefs
        row = (cell_ref[:, cols] // 256).astype(f32)
        col = (cell_ref[:, cols] % 256).astype(f32)
        here = slot_number == rank

        def spread_out(coef, single):
            parts = [jnp.where(rank == d, coef, 0.0) for d in range(SLOTS)]
            parts += [jnp.where(here, value, 0.0) for value in single]
            parts.append(jnp.zeros((SLOTS * (4 - len(single)), BLOCK), f32))
            return jnp.concatenate(parts, 0).astype(bf16)

        coef_high = coefs.astype(bf16).astype(f32)
        constant_high = constant.astype(bf16).astype(f32)
        payload[...] += nt(mark, spread_out(coef_high, (constant_high, row, col))) + nt(
            mark, spread_out(coefs - coef_high, (constant - constant_high,))
        )
        return used

    blocks = count // BLOCK
    used = lax.fori_loop(0, blocks // 2, list_block, jnp.zeros((tiles, 1), f32))

    def along_x(k):
        return lax.rem(gx + k, n_gx)

    def along_y(k):
        return lax.rem(gy + k, n_gy)

    def stage_x(source_of, target, send_sem, recv_sem):
        copies = []
        for k in range(1, n_gx):
            peer = along_x(k)
            copy = pltpu.make_async_remote_copy(
                src_ref=source_of(peer),
                dst_ref=target.at[gx],
                send_sem=send_sem.at[k],
                recv_sem=recv_sem.at[k],
                device_id=(peer, gy),
                device_id_type=MESH,
            )
            copy.start()
            copies.append(copy)
        return copies

    def stage_y(source_of, target, send_sem, recv_sem):
        copies = []
        for k in range(1, n_gy):
            peer = along_y(k)
            copy = pltpu.make_async_remote_copy(
                src_ref=source_of(peer),
                dst_ref=target.at[gy],
                send_sem=send_sem.at[k],
                recv_sem=recv_sem.at[k],
                device_id=(gx, peer),
                device_id_type=MESH,
            )
            copy.start()
            copies.append(copy)
        return copies

    def arrived_x(target, send_sem, recv_sem):
        for k in range(1, n_gx):
            place = target.at[lax.rem(gx + n_gx - k, n_gx)]
            pltpu.make_async_remote_copy(
                src_ref=place,
                dst_ref=place,
                send_sem=send_sem.at[k],
                recv_sem=recv_sem.at[k],
                device_id=(along_x(k), gy),
                device_id_type=MESH,
            ).wait_recv()

    def arrived_y(target, send_sem, recv_sem):
        for k in range(1, n_gy):
            place = target.at[lax.rem(gy + n_gy - k, n_gy)]
            pltpu.make_async_remote_copy(
                src_ref=place,
                dst_ref=place,
                send_sem=send_sem.at[k],
                recv_sem=recv_sem.at[k],
                device_id=(gx, along_y(k)),
                device_id_type=MESH,
            ).wait_recv()

    for copy in loads[6:]:
        copy.wait()
    soil_step(0)
    lax.fori_loop(blocks // 2, blocks, list_block, used)
    sends = []
    sends += stage_x(
        lambda peer: payload.at[pl.ds(pl.multiple_of(peer * n_gy, n_gy), n_gy)],
        recv_one,
        one_send,
        one_recv,
    )
    recv_one[gx] = payload[pl.ds(pl.multiple_of(gx * n_gy, n_gy), n_gy), :]

    for side in range(2):

        @pl.when(has[side])
        def _():
            for copy in cone_x(side, True):
                copy.wait_recv()

    cone_edges()
    for side in range(2):

        @pl.when(has[2 + side])
        def _():
            cone_y(side).start()

    soil_step(1)

    arrived_x(recv_one, one_send, one_recv)
    for q in range(n_gy):
        for s in range(n_gx):
            mid_one[q, pl.ds(s, 1), :] = recv_one[s, pl.ds(q, 1), :]
    sends += stage_y(lambda peer: mid_one.at[peer], request, two_send, two_recv)
    request[gy] = mid_one[gy]

    soil_step(2)

    for side in range(2):

        @pl.when(has[2 + side])
        def _():
            cone_y(side, True).wait_recv()

    cone_sides()
    cone_steps()
    soil_step(3)

    arrived_y(request, two_send, two_recv)
    for q in range(WIDE // 128):
        request_t[pl.ds(q * 128, 128), :] = (
            request[:, :, pl.ds(q * 128, 128)].reshape(tiles, 128).T
        )
    table = jnp.concatenate(split(jnp.concatenate([motion[0], motion[1]], 1)), 1)
    line_number = lax.broadcasted_iota(jnp.int32, (rows, 128), 0).astype(f32)

    column_number = lax.broadcasted_iota(jnp.int32, (256, 128), 0).astype(f32)
    LINES = 4

    def pick(group, unused):
        chosen = []
        for i in range(LINES):
            wanted = request_t[pl.ds(COL + group * LINES + i, 1), :]
            chosen.append((column_number == wanted).astype(f32).astype(bf16))
        chosen = jnp.concatenate(chosen, 1)
        hot[:, pl.ds(pl.multiple_of(group * LINES * 128, 128), LINES * 128)] = chosen
        found = nn(table, jnp.concatenate([chosen, chosen], 0))
        totals = []
        for i in range(LINES):
            wanted = request_t[pl.ds(ROW + group * LINES + i, 1), :]
            sums = [jnp.zeros((STEPS, 128), f32) for unused_part in range(4)]
            for r in range(rows):
                sums[r % 4] += jnp.where(
                    wanted == float(r),
                    found[r * STEPS : (r + 1) * STEPS, i * 128 : (i + 1) * 128],
                    0.0,
                )
            totals.append((sums[0] + sums[1]) + (sums[2] + sums[3]))
        size = LINES * STEPS
        picked[pl.ds(pl.multiple_of(group * size, size), size), :] = jnp.concatenate(totals, 0)
        return unused

    lax.fori_loop(0, SLOTS // LINES, pick, 0)
    for q in range(2):
        reply[:, :, pl.ds(q * 128, 128)] = (
            picked[pl.ds(q * 128, 128), :].T.reshape(n_gy, n_gx, 128)
        )
    sends += stage_y(lambda peer: reply.at[peer], recv_two, three_send, three_recv)
    recv_two[gy] = reply[gy]

    stores = []
    soil_step(4)

    LANDED = 8

    def land(group, total):
        cols = pl.ds(pl.multiple_of(group * LANDED * 128, 128), LANDED * 128)
        parts = []
        for i in range(LANDED):
            d = group * LANDED + i
            lines = pl.ds(pl.multiple_of(d * STEPS, STEPS), STEPS)
            mean = request_t[pl.ds(BASE + d, 1), :] + jnp.sum(
                request_t[lines, :] * picked[lines, :], 0, keepdims=True
            )
            parts.append(jnp.where(line_number == request_t[pl.ds(ROW + d, 1), :], mean, 0.0))
        values = jnp.concatenate(parts, 1)
        return total + nt(jnp.concatenate(split(values), 0), hot[:, cols])

    landed = lax.fori_loop(0, SLOTS // LANDED, land, jnp.zeros((2 * rows, 256), f32))
    base[...] = landed[:rows] + landed[rows:]
    stores.append(pltpu.make_async_copy(base, base_out, out_sem.at[0]))
    stores[-1].start()

    soil_step(5)
    arrived_y(recv_two, three_send, three_recv)
    for s in range(n_gx):
        for q in range(n_gy):
            mid_two[s, pl.ds(q, 1), :] = recv_two[q, pl.ds(s, 1), :]
    sends += stage_x(lambda peer: mid_two.at[peer], answer, four_send, four_recv)
    answer[gx] = mid_two[gx]
    soil_step(6)

    def store(source, target):
        stores.append(pltpu.make_async_copy(source, target, out_sem.at[len(stores)]))
        stores[-1].start()

    for i in range(2):
        store(
            states[(STEPS + 1) % 2].at[i, pl.ds(PAD, cells)],
            before_hbm.at[:, pl.ds(i * 128, 128)],
        )
    for side in range(2):

        @pl.when(has[side])
        def _():
            for copy in cone_x(side):
                copy.wait_send()

        @pl.when(has[2 + side])
        def _():
            cone_y(side).wait_send()

    for slot in range(STEPS):
        for part in range(CHUNKS):
            for side in range(4):

                @pl.when(has[side])
                def _():
                    halo(slot, part, side).wait_send()

    sent = len(sends) - (n_gx - 1)
    for copy in sends[:sent]:
        copy.wait_send()
    arrived_x(answer, four_send, four_recv)

    answer_t = jnp.concatenate(
        [answer[:, :, pl.ds(q * 128, 128)].reshape(tiles, 128).T for q in range(2)], 0
    )
    decoded = jnp.concatenate(split(answer_t), 1)
    level = lax.broadcasted_iota(jnp.int32, (32, BLOCK), 0)

    def window(j, unused):
        cols = pl.ds(pl.multiple_of(j * BLOCK, BLOCK), BLOCK)
        mark = marks[:, cols]
        found = nn(decoded, jnp.concatenate([mark, mark], 0))
        rank = rank_ref[:, cols]
        ground = jnp.zeros((STEPS, BLOCK), f32)
        for d in range(SLOTS):
            ground += jnp.where(rank == d, found[d * STEPS : (d + 1) * STEPS], 0.0)
        k, place, speed = stiff[:, cols], disp[:, cols], vel[:, cols]
        for step in range(STEPS):
            beneath = jnp.where(level == 0, ground[step : step + 1], pltpu.roll(place, 1, 0))
            shear = k * (place - beneath)
            upper = jnp.where(level == 31, 0.0, pltpu.roll(shear, 31, 0))
            speed = speed + upper - shear
            place = place + speed
        disp_new[:, cols] = place
        vel_new[:, cols] = speed
        return unused

    lax.fori_loop(0, count // BLOCK, window, 0)
    store(disp_new, disp_out)
    store(vel_new, vel_out)

    for part in range(CHUNKS):
        advance(STEPS - 1, part)
        for i in range(2):
            first, size = part * planes * rows, planes * rows
            store(
                states[STEPS % 2].at[i, pl.ds(PAD + first, size)],
                next_hbm.at[pl.ds(first, size), pl.ds(i * 128, 128)],
            )
    for copy in sends[sent:]:
        copy.wait_send()

    for copy in stores:
        copy.wait()


def hand_over(*refs):
    sources, targets, held, sems = refs[:5], refs[5:10], refs[10:15], refs[15:]
    ways = []
    for source, target, room in zip(sources, targets, held):
        pieces = 6 if source.shape[0] > 256 else 1
        size = source.shape[0] // pieces
        for i in range(pieces):
            part = pl.ds(i * size, size)
            ways.append((source.at[part], room.at[part], target.at[part]))
    reads = [pltpu.make_async_copy(a, b, sems[0].at[i]) for i, (a, b, c) in enumerate(ways)]
    writes = [pltpu.make_async_copy(b, c, sems[1].at[i]) for i, (a, b, c) in enumerate(ways)]
    for copy in reads:
        copy.start()
    for read, write in zip(reads, writes):
        read.wait()
        write.start()
    for copy in writes:
        copy.wait()


def shards(
    soil_now,
    soil_old,
    kappa,
    force_prev,
    storey_disp,
    storey_vel,
    stiffness,
    branch_flag,
    footprint_tile,
    footprint_cell,
):
    n_gx, n_gy = lax.axis_size("gx"), lax.axis_size("gy")
    depth, rows, wide = soil_now.shape
    storeys, count = storey_disp.shape
    tiles = n_gx * n_gy
    flat = (depth * rows, wide)
    around = rows + 2 * STEPS
    hbm = pl.BlockSpec(memory_space=pltpu.HBM)
    dma = pltpu.SemaphoreType.DMA
    vm = pltpu.VMEM
    out = pl.pallas_call(
        functools.partial(kernel, n_gx, n_gy, depth, rows),
        out_shape=(
            jax.ShapeDtypeStruct(flat, f32),
            jax.ShapeDtypeStruct(flat, f32),
            jax.ShapeDtypeStruct((storeys, count), f32),
            jax.ShapeDtypeStruct((storeys, count), f32),
            jax.ShapeDtypeStruct((rows, wide), f32),
        ),
        in_specs=[pl.BlockSpec(memory_space=pltpu.VMEM)] * 2 + [hbm] * 11,
        out_specs=(hbm,) * 5,
        scratch_shapes=[
            vm((2, PAD + flat[0] + rows, 128), f32),
            vm((2, PAD + flat[0] + rows, 128), f32),
            vm((2, PAD + flat[0], 128), f32),
            vm((rows, wide), f32),
            vm((storeys, count), f32),
            vm((storeys, count), f32),
            vm((storeys, count), f32),
            vm((storeys, count), jnp.int32),
            vm((storeys, count), f32),
            vm((storeys, count), f32),
            vm((rows, wide), f32),
            vm((STEPS, 2, 2, depth, 128), f32),
            vm((STEPS, 2, 2, depth, 128), f32),
            vm((STEPS, CHUNKS, rows, 128), f32),
            vm((STEPS, CHUNKS, 2, rows, 128), f32),
            vm((STEPS + 1, around, 384), f32),
            vm((STEPS, around, 384), f32),
            vm((STEPS, around, 384), f32),
            vm((around, 384), f32),
            vm((2, 2, around, 128), f32),
            vm((2, 2, around, 128), f32),
            vm((tiles, count), bf16),
            vm((1, count), jnp.int32),
            vm((tiles, WIDE), f32),
            vm((n_gx, n_gy, WIDE), f32),
            vm((n_gy, n_gx, WIDE), f32),
            vm((n_gy, n_gx, WIDE), f32),
            vm((WIDE, tiles), f32),
            vm((wide, SLOTS * tiles), bf16),
            vm((2, rows * STEPS, 128), f32),
            vm((SLOTS * STEPS, tiles), f32),
            vm((n_gy, n_gx, SLOTS * STEPS), f32),
            vm((n_gy, n_gx, SLOTS * STEPS), f32),
            vm((n_gx, n_gy, SLOTS * STEPS), f32),
            vm((n_gx, n_gy, SLOTS * STEPS), f32),
            dma((15,)),
            dma((9,)),
            dma((STEPS, CHUNKS, 4)),
            dma((STEPS, CHUNKS, 4)),
            dma((4, 2)),
            dma((4, 2)),
            dma((2,)),
            dma((2,)),
            dma((n_gx,)),
            dma((n_gx,)),
            dma((n_gy,)),
            dma((n_gy,)),
            dma((n_gy,)),
            dma((n_gy,)),
            dma((n_gx,)),
            dma((n_gx,)),
        ],
        compiler_params=pltpu.CompilerParams(
            collective_id=0, has_side_effects=True, vmem_limit_bytes=62 * 1024 * 1024
        ),
        cost_estimate=pl.CostEstimate(
            flops=4_000_000_000, bytes_accessed=10_000_000, transcendentals=0
        ),
    )(
        footprint_tile.reshape(1, count),
        footprint_cell.reshape(1, count),
        soil_now.reshape(flat),
        soil_old.reshape(flat),
        kappa.reshape(flat),
        soil_now,
        soil_old,
        kappa,
        force_prev,
        storey_disp,
        storey_vel,
        stiffness,
        branch_flag,
    )
    out = pl.pallas_call(
        hand_over,
        out_shape=tuple(jax.ShapeDtypeStruct(a.shape, a.dtype) for a in out),
        in_specs=[hbm] * 5,
        out_specs=(hbm,) * 5,
        scratch_shapes=[vm(a.shape, a.dtype) for a in out] + [dma((15,)), dma((15,))],
        compiler_params=pltpu.CompilerParams(vmem_limit_bytes=62 * 1024 * 1024),
    )(*out)
    return (
        out[0].reshape(soil_now.shape),
        out[1].reshape(soil_now.shape),
        out[2],
        out[3],
        out[4],
    )


def solution(mesh):
    return jax.shard_map(
        shards,
        mesh=mesh,
        in_specs=(
            P(None, "gx", "gy"),
            P(None, "gx", "gy"),
            P(None, "gx", "gy"),
            P("gx", "gy"),
            P(None, ("gx", "gy")),
            P(None, ("gx", "gy")),
            P(None, ("gx", "gy")),
            P(None, ("gx", "gy")),
            P(("gx", "gy"), None),
            P(("gx", "gy")),
        ),
        out_specs=(
            P(None, "gx", "gy"),
            P(None, "gx", "gy"),
            P(None, ("gx", "gy")),
            P(None, ("gx", "gy")),
            P("gx", "gy"),
        ),
        check_vma=False,
    )
```
